512 devices in a mesh: frame: 16 (over z, core), row: 32 (over y, x).
Axes of the slice: x: 4, y: 8, z: 8, core: 2. Of those that a mesh axis runs over, the one named last changes fastest.
Arguments:
- features: bfloat16 [32, 128, 24, 256], P('frame', 'row'), may hold values from -12 to 12
- norm_gain: float32 [256], replicated, may hold values from 0.5 to 2
- conv_up: bfloat16 [3, 3, 3, 256, 256], replicated, may hold values from -0.078125 to 0.078125
Outputs:
- decoded: bfloat16 [64, 256, 48, 256], P('frame', 'row')
The draws below stay inside these ranges and needn't reach their ends.
All inputs are finite; a program needn't handle non-finite values.
Results may differ from the reference program's by a relative error of at most 0.0049.
Values may be sent and summed in bfloat16 or wider, within the bound.
A program may use at most 64 MiB of HBM per device.

```python
import math
import jax
import jax.numpy as jnp
from jax import lax

C = 256
GROUPS = 32
COLS = 24
NT = 32
NH = 128


def draw_features(key, part):
    key = jax.random.fold_in(key, 11)
    key_base = jax.random.fold_in(key, 0)
    key_rough = jax.random.fold_in(key, 1)
    key_cell = jax.random.fold_in(key, 3)
    key_shift = jax.random.fold_in(key, 4)
    shape_all = (NT, NH, COLS, C)
    frame_pos = jnp.arange(NT, dtype=jnp.float32) / (NT - 1)
    row_pos = jnp.arange(NH, dtype=jnp.float32) / (NH - 1)
    ramp = jnp.sqrt(1.0 + 2.0 * frame_pos)[:, None, None, None] * jnp.sqrt(1.0 + 2.0 * row_pos)[None, :, None, None]
    rough = jnp.exp(jax.random.uniform(key_rough, shape_all, jnp.float32, -0.35, 0.35))
    cell_scale = jnp.exp(jax.random.uniform(key_cell, (NT, NH, 1, 1), jnp.float32, -0.7, 0.7))
    base = jax.random.normal(key_base, shape_all, jnp.float32)
    shift = jax.random.normal(key_shift, (NT, NH, 1, GROUPS), jnp.float32)
    shift_chan = jnp.repeat(shift, C // GROUPS, axis=3)
    value = ramp * (0.6 * base * rough * cell_scale + shift_chan)
    return jnp.clip(value, -12.0, 12.0).astype(jnp.bfloat16)


def normal_values(rng, extent, scale, reach, kind=jnp.bfloat16):
    return jnp.clip(scale * jax.random.normal(rng, extent, jnp.float32), -reach, reach).astype(kind)


def setup_inputs(seed: int = 0) -> dict:
    arg_keys = jax.random.split(jax.random.key(seed), 4)
    return {
        "features": draw_features(jax.random.fold_in(arg_keys[3], 71), 0),
        "norm_gain": jnp.clip(jnp.exp(jax.random.uniform(arg_keys[1], (C,), jnp.float32, math.log(0.5), math.log(2.0))), 0.5, 2.0),
        "conv_up": normal_values(arg_keys[2], (3, 3, 3, C, C), (27 * C) ** -0.5, 0.078125),
    }


def edge_pad(volume, depth):
    leading = jnp.concatenate([volume[:1]] * depth + [volume], 0)
    leading = jnp.concatenate([leading[:, :1], leading, leading[:, -1:]], 1)
    return jnp.concatenate([leading[:, :, :1], leading, leading[:, :, -1:]], 2)

def causal_conv(volume, weight):
    padded = edge_pad(volume, 2)
    height = volume.shape[1]
    widths = volume.shape[2]

    def one_frame(index):
        slab = lax.dynamic_slice_in_dim(padded, index, 3, 0)
        running = jnp.zeros((height * widths, weight.shape[4]), jnp.float32)
        for tap_t in range(3):
            for tap_h in range(3):
                for tap_w in range(3):
                    window = slab[tap_t, tap_h:tap_h + height, tap_w:tap_w + widths].reshape(-1, weight.shape[3])
                    running = running + jnp.dot(window, weight[tap_t, tap_h, tap_w], preferred_element_type=jnp.float32)
        return running.reshape(height, widths, -1).astype(jnp.bfloat16)
    return lax.map(one_frame, jnp.arange(volume.shape[0], dtype=jnp.int32))

def reference(features, norm_gain, conv_up):
    chan_count = features.shape[3]
    group_size = chan_count // GROUPS
    values = features.astype(jnp.float32).reshape(-1, GROUPS, group_size)
    group_mean = lax.optimization_barrier(jnp.mean(values, axis=(0, 2)))
    group_var = lax.optimization_barrier(jnp.mean(jnp.square(values - group_mean[None, :, None]), axis=(0, 2)))
    mean_chan = jnp.repeat(group_mean, group_size)
    inv_chan = jnp.repeat(lax.rsqrt(group_var + 1e-06), group_size)
    activated = jax.nn.silu((features.astype(jnp.float32) - mean_chan) * inv_chan * norm_gain).astype(jnp.bfloat16)
    upsampled = jnp.repeat(jnp.repeat(jnp.repeat(activated, 2, 0), 2, 1), 2, 2)
    return causal_conv(upsampled, conv_up)
```

```python
import functools

import jax
import jax.numpy as jnp
from jax import lax
from jax.experimental import pallas as pl
from jax.experimental.pallas import tpu as pltpu
from jax.sharding import PartitionSpec as P

MESH = pl.DeviceIdType.MESH
GROUP = 8
F32, BF16 = jnp.float32, jnp.bfloat16


def lane_index(shape):
    return lax.broadcasted_iota(jnp.int32, shape, len(shape) - 1)


def swapped(value, distance):
    upper = (lane_index(value.shape) & distance) == 0
    return jnp.where(upper, pltpu.roll(value, 128 - distance, 1), pltpu.roll(value, distance, 1))


def local_statistics(own, rows):
    count = float(rows)
    mean = jnp.sum(own, axis=0, keepdims=True) * (1.0 / count)
    spread = jnp.sum(jnp.square(own - mean), axis=0, keepdims=True)
    packed = jnp.zeros((8, 128), F32)
    kind = lane_index((8, 128)) & 7
    for half in range(2):
        lanes = slice(128 * half, 128 * half + 128)
        m = jnp.broadcast_to(mean[:, lanes], (8, 128))
        s = jnp.broadcast_to(spread[:, lanes], (8, 128))
        held = count
        for distance in (1, 2, 4):
            other_m, other_s = swapped(m, distance), swapped(s, distance)
            s = s + other_s + (0.5 * held) * jnp.square(m - other_m)
            m = 0.5 * (m + other_m)
            held *= 2.0
        packed = jnp.where(kind == half, m, jnp.where(kind == 2 + half, s, packed))
    return packed[0:1]


def merged(parts, count):
    total = jnp.sum(parts, axis=0)
    mean = total * (1.0 / parts.shape[0])
    apart = jnp.sum(jnp.square(parts - mean[None]), axis=0)
    apart = pltpu.roll(jnp.broadcast_to(apart, (8, 128)), 2, 1)[0:1]
    kind = lane_index((1, 128)) & 7
    return jnp.where(kind < 2, mean, total + count * apart)


def comm_kernel(
    shape, feat, weight, gain, halo_out, stat_out, folded,
    raw, held, scale, msg1, buf1, msg2, buf2, in_sem, send1, recv1, send2, recv2, halo_send, halo_recv,
):
    frames, ydim, xdim, total = shape
    rows = ydim * xdim
    f, r = lax.axis_index("frame"), lax.axis_index("row")
    y, x = r // xdim, r % xdim
    own = held.at[1:3, 48:144]

    load = pltpu.make_async_copy(feat, own, in_sem.at[0])
    load.start()

    def plane(i):
        return ((y + i // xdim) % ydim) * xdim + (x + i) % xdim

    barrier = pltpu.get_barrier_semaphore()

    def greet_plane(i, carry):
        pl.semaphore_signal(barrier, inc=1, device_id=(f, plane(i)), device_id_type=MESH)
        return carry

    def greet_later(k, carry):
        pl.semaphore_signal(barrier, inc=1, device_id=(k, r), device_id_type=MESH)
        return carry

    lax.fori_loop(f + 1, frames, greet_later, 0)
    lax.fori_loop(1, rows, greet_plane, 0)

    fetch = pltpu.make_async_copy(weight, raw, in_sem.at[1])
    fetch.start()
    gains = pltpu.make_async_copy(gain, scale, in_sem.at[2])
    gains.start()

    load.wait()
    values = held[1:3, 48:144].astype(F32).reshape(192, 256)
    mine = local_statistics(values, 192)
    msg1[...] = mine
    buf1[f] = mine
    pl.semaphore_wait(barrier, rows - 1 + f)

    def send_first(k, carry):
        pltpu.make_async_remote_copy(
            src_ref=msg1, dst_ref=buf1.at[f], send_sem=send1, recv_sem=recv1.at[f],
            device_id=(k, r), device_id_type=MESH,
        ).start()
        return carry

    lax.fori_loop(0, f, send_first, 0)

    down = pltpu.make_async_remote_copy(
        src_ref=held.at[1:3, 96:144], dst_ref=held.at[1:3, 0:48], send_sem=halo_send.at[0],
        recv_sem=halo_recv.at[0], device_id=(f, (r + 1) % rows), device_id_type=MESH,
    )
    up = pltpu.make_async_remote_copy(
        src_ref=held.at[1:3, 48:96], dst_ref=held.at[1:3, 144:192], send_sem=halo_send.at[1],
        recv_sem=halo_recv.at[1], device_id=(f, (r + rows - 1) % rows), device_id_type=MESH,
    )
    down.start()
    up.start()

    fetch.wait()
    gains.wait()

    def fold(step, carry):
        at = pl.multiple_of(step * 16, 16)
        for half in range(2):
            lanes = slice(128 * half, 128 * half + 128)
            for kind in range(3):
                def tap(h, w):
                    if kind == 0:
                        return raw[h * 3 + w, pl.ds(at, 16), lanes].astype(F32) + raw[
                            9 + h * 3 + w, pl.ds(at, 16), lanes].astype(F32)
                    return raw[(18 if kind == 1 else 9) + h * 3 + w, pl.ds(at, 16), lanes].astype(F32)

                t = [[tap(h, w) for w in range(3)] for h in range(3)]
                by_row = [[t[0], [t[1][w] + t[2][w] for w in range(3)]],
                          [[t[0][w] + t[1][w] for w in range(3)], t[2]]]
                for p in range(2):
                    for a in range(2):
                        u = by_row[p][a]
                        by_col = [[u[0], u[1] + u[2]], [u[0] + u[1], u[2]]]
                        for q in range(2):
                            for b in range(2):
                                base = kind * 1024 + (a * 2 + b) * 256
                                folded[p * 2 + q, pl.ds(base + at, 16), lanes] = by_col[q][b].astype(BF16)
        return carry

    lax.fori_loop(0, 16, fold, 0)

    def answer(k, carry):
        pltpu.make_async_copy(buf1.at[k], buf1.at[k], recv1.at[k]).wait()
        pltpu.make_async_remote_copy(
            src_ref=msg1, dst_ref=buf1.at[f], send_sem=send1, recv_sem=recv1.at[f],
            device_id=(k, r), device_id_type=MESH,
        ).start()
        return carry

    lax.fori_loop(f + 1, frames, answer, 0)
    down.wait_recv()
    up.wait_recv()
    forward = pltpu.make_async_remote_copy(
        src_ref=held.at[2], dst_ref=held.at[0], send_sem=halo_send.at[2], recv_sem=halo_recv.at[2],
        device_id=((f + 1) % frames, r), device_id_type=MESH,
    )

    @pl.when(f + 1 < frames)
    def _():
        forward.start()

    def collect(k, carry):
        pltpu.make_async_copy(buf1.at[k], buf1.at[k], recv1.at[k]).wait()
        return carry

    lax.fori_loop(0, f, collect, 0)
    line = merged(buf1[...], 192.0 * GROUP)
    msg2[...] = line
    buf2[r] = line

    def send_second(i, carry):
        pltpu.make_async_remote_copy(
            src_ref=msg2, dst_ref=buf2.at[r], send_sem=send2, recv_sem=recv2,
            device_id=(f, plane(i)), device_id_type=MESH,
        ).start()
        return carry

    lax.fori_loop(rows // 2, rows, send_second, 0)
    lax.fori_loop(1, rows // 2, send_second, 0)

    @pl.when(f > 0)
    def _():
        forward.wait_recv()

    @pl.when(f == 0)
    def _():
        held[0] = held[1]

    halo_out[...] = held[...]
    others = buf2.at[0:rows - 1]
    pltpu.make_async_copy(others, others, recv2).wait()
    line = jnp.broadcast_to(merged(buf2[...], 192.0 * GROUP * frames), (8, 128))
    kind = lane_index((8, 128)) & 7
    spread = []
    for k in range(4):
        v = jnp.where(kind == k, line, 0.0)
        for distance in (1, 2, 4):
            v = v + swapped(v, distance)
        spread.append(v[0:1])
    var = jnp.concatenate(spread[2:], axis=1) * (1.0 / total)
    stat_out[0:1] = jnp.concatenate(spread[:2], axis=1)
    stat_out[1:2] = lax.rsqrt(var + 1e-06) * scale[...]

    sent = buf1.at[0:frames - 1]
    pltpu.make_async_copy(sent, sent, send1).wait()
    pltpu.make_async_copy(others, others, send2).wait()
    down.wait_send()
    up.wait_send()

    @pl.when(f + 1 < frames)
    def _():
        forward.wait_send()


def conv_kernel(shape, halo, stat, folded, out, act, even_rows, odd_rows, wide, staged, out_sem):
    rows = shape
    r = lax.axis_index("row")

    mean, scale = stat[0:1], stat[1:2]
    for t in range(3):
        v = (halo[t, :, :].astype(F32)[24:168] - mean) * scale
        v = (v / (1.0 + jnp.exp(-v))).astype(BF16).astype(F32).reshape(6, 24, 256)
        top = jnp.where(r == 0, v[1:2], v[0:1])
        bottom = jnp.where(r == rows - 1, v[4:5], v[5:6])
        v = jnp.concatenate([top, v[1:5], bottom], axis=0)
        act[t, :, 8:32, :] = v
        act[t, :, 7:8, :] = v[:, 0:1]
        act[t, :, 32:33, :] = v[:, 23:24]
    for s in range(3):
        v = [act[t, :, 7 + s:31 + s, :] for t in range(3)]
        v = v + [v[1] - v[0], v[2] - v[1]]
        for t in range(5):
            even_rows[s, t] = v[t].reshape(144, 256).astype(BF16)
            odd_rows[s, t] = v[t][1:5].reshape(96, 256).astype(BF16)

    def piece(kind, sr, sc):
        first = (0, 1, 3)[kind]
        if sr == 1:
            return odd_rows[sc, first:first + 2].reshape(192, 256)
        return even_rows[sc, first:first + 2, 24 * sr:24 * sr + 96].reshape(192, 256)

    copies = []
    for p in range(2):
        for q in range(2):
            def taps(kind):
                return [piece(kind, p + a, q + b) for a in range(2) for b in range(2)]

            first = jnp.dot(jnp.concatenate(taps(0) + taps(1), axis=1), folded[p * 2 + q, 0:2048],
                            preferred_element_type=F32)
            step = jnp.dot(jnp.concatenate(taps(2), axis=1), folded[p * 2 + q, 2048:3072],
                           preferred_element_type=F32)
            second = first + step
            for i in range(2):
                for alpha, v in enumerate((first, second)):
                    for half in range(2):
                        lanes = slice(128 * half, 128 * half + 128)
                        wide[half, 2 * i + alpha, :, pl.ds(q, 24, 2), :] = v[96 * i:96 * i + 96, lanes].reshape(
                            4, 24, 128)
        for half in range(2):
            staged[p, :, :, :, 128 * half:128 * half + 128] = wide[half].astype(BF16)
        copy = pltpu.make_async_copy(staged.at[p], out.at[:, :, p], out_sem.at[p])
        copy.start()
        copies.append(copy)
    for copy in copies:
        copy.wait()


def solution(mesh):
    frames, rows = mesh.shape["frame"], mesh.shape["row"]
    xdim = 4 if rows % 4 == 0 else 1
    any_, vmem = pl.BlockSpec(memory_space=pltpu.HBM), pl.BlockSpec(memory_space=pltpu.VMEM)

    def shards(features, norm_gain, conv_up):
        voxels = float(192 * GROUP * frames * rows)
        halo, stat, folded = pl.pallas_call(
            functools.partial(comm_kernel, (frames, rows // xdim, xdim, voxels)),
            out_shape=(pltpu.VMEM((3, 192, 256), BF16), pltpu.VMEM((2, 256), F32), pltpu.VMEM((4, 3072, 256), BF16)),
            in_specs=[any_, any_, any_],
            out_specs=(vmem, vmem, vmem),
            scratch_shapes=[
                pltpu.VMEM((27, 256, 256), BF16),
                pltpu.VMEM((3, 192, 256), BF16),
                pltpu.VMEM((1, 256), F32),
                pltpu.VMEM((1, 128), F32),
                pltpu.VMEM((frames, 1, 128), F32),
                pltpu.VMEM((1, 128), F32),
                pltpu.VMEM((rows, 1, 128), F32),
                pltpu.SemaphoreType.DMA((3,)),
                pltpu.SemaphoreType.DMA,
                pltpu.SemaphoreType.DMA((frames,)),
                pltpu.SemaphoreType.DMA,
                pltpu.SemaphoreType.DMA,
                pltpu.SemaphoreType.DMA((3,)),
                pltpu.SemaphoreType.DMA((3,)),
            ],
            compiler_params=pltpu.CompilerParams(
                collective_id=0, has_side_effects=True, vmem_limit_bytes=54 * 2**20),
            name="statistics",
        )(features.reshape(2, 96, 256), conv_up.reshape(27, 256, 256), norm_gain.reshape(1, 256))
        out = pl.pallas_call(
            functools.partial(conv_kernel, rows),
            out_shape=jax.ShapeDtypeStruct((4, 4, 2, 48, 256), BF16),
            in_specs=[vmem, vmem, vmem],
            out_specs=any_,
            scratch_shapes=[
                pltpu.VMEM((3, 6, 40, 256), F32),
                pltpu.VMEM((3, 5, 144, 256), BF16),
                pltpu.VMEM((3, 5, 96, 256), BF16),
                pltpu.VMEM((2, 4, 4, 48, 128), F32),
                pltpu.VMEM((2, 4, 4, 48, 256), BF16),
                pltpu.SemaphoreType.DMA((2,)),
            ],
            compiler_params=pltpu.CompilerParams(vmem_limit_bytes=24 * 2**20),
            name="conv",
        )(halo, stat, folded)
        return out.reshape(4, 8, 48, 256)

    spec = P("frame", "row", None, None)
    return jax.shard_map(shards, mesh=mesh, in_specs=(spec, P(), P()), out_specs=spec, check_vma=False)
```

```python
import functools

import jax
import jax.numpy as jnp
from jax import lax
from jax.experimental import pallas as pl
from jax.experimental.pallas import tpu as pltpu
from jax.sharding import PartitionSpec as P

MESH = pl.DeviceIdType.MESH
GROUP = 8
F32, BF16 = jnp.float32, jnp.bfloat16
ROOT = 1
LATE = 6


def lane_index(shape):
    return lax.broadcasted_iota(jnp.int32, shape, len(shape) - 1)


def swapped(value, distance):
    upper = (lane_index(value.shape) & distance) == 0
    return jnp.where(upper, pltpu.roll(value, 128 - distance, 1), pltpu.roll(value, distance, 1))


def local_statistics(own, rows):
    count = float(rows)
    mean = jnp.sum(own, axis=0, keepdims=True) * (1.0 / count)
    spread = jnp.sum(jnp.square(own - mean), axis=0, keepdims=True)
    packed = jnp.zeros((8, 128), F32)
    kind = lane_index((8, 128)) & 7
    for half in range(2):
        lanes = slice(128 * half, 128 * half + 128)
        m = jnp.broadcast_to(mean[:, lanes], (8, 128))
        s = jnp.broadcast_to(spread[:, lanes], (8, 128))
        held = count
        for distance in (1, 2, 4):
            other_m, other_s = swapped(m, distance), swapped(s, distance)
            s = s + other_s + (0.5 * held) * jnp.square(m - other_m)
            m = 0.5 * (m + other_m)
            held *= 2.0
        packed = jnp.where(kind == half, m, jnp.where(kind == 2 + half, s, packed))
    return packed[0:1]


def merged(parts, count):
    total = jnp.sum(parts, axis=0)
    mean = total * (1.0 / parts.shape[0])
    apart = jnp.sum(jnp.square(parts - mean[None]), axis=0)
    apart = pltpu.roll(jnp.broadcast_to(apart, (8, 128)), 2, 1)[0:1]
    kind = lane_index((1, 128)) & 7
    return jnp.where(kind < 2, mean, total + count * apart)


def comm_kernel(
    shape, feat, weight, gain, halo_out, stat_out, folded,
    raw, held, scale, msg1, buf1, lines, final,
    in_sem, send1, recv1, send3, recv3, halo_send, halo_recv, ready,
):
    frames, ydim, xdim, total = shape
    rows = ydim * xdim
    f, r = lax.axis_index("frame"), lax.axis_index("row")
    y, x = r // xdim, r % xdim
    is_root = f == ROOT

    loads = [
        pltpu.make_async_copy(feat.at[t, part], held.at[1 + t, pl.ds(48 + part.start, 48)], in_sem.at[2 + 2 * t + i])
        for t in range(2) for i, part in enumerate((slice(0, 48), slice(48, 96)))
    ]
    for load in loads:
        load.start()

    def order(row):
        return row % xdim * rows + row

    below, above = (r + 1) % rows, (r + rows - 1) % rows
    below_later, above_later = order(below) > order(r), order(above) > order(r)

    def plane(i):
        return ((y + i // xdim) % ydim) * xdim + (x + i) % xdim

    def to_root(i):
        return pltpu.make_async_remote_copy(
            src_ref=msg1, dst_ref=buf1.at[f, r], send_sem=send1, recv_sem=recv1.at[f],
            device_id=(ROOT, plane(i)), device_id_type=MESH,
        )

    barrier = pltpu.get_barrier_semaphore()

    def greet(frame, row):
        pl.semaphore_signal(barrier, inc=1, device_id=(frame, row), device_id_type=MESH)

    def greet_plane(i, carry):
        greet(f, plane(i))
        return carry

    def greet_line(k, carry):
        greet(k, r)
        return carry

    @pl.when(is_root)
    def _():
        lax.fori_loop(1, rows, greet_plane, 0)

    @pl.when(jnp.logical_not(is_root))
    def _():
        @pl.when(below_later)
        def _():
            greet(f, below)

        @pl.when(above_later)
        def _():
            greet(f, above)

    for load in loads:
        load.wait()
    values = held[1:3, 48:144].astype(F32).reshape(192, 256)
    mine = local_statistics(values, 192)
    msg1[...] = mine
    pl.semaphore_wait(barrier, jnp.where(
        is_root, rows - 1, 3 - below_later.astype(jnp.int32) - above_later.astype(jnp.int32)))

    @pl.when(is_root)
    def _():
        buf1[ROOT, r] = mine
        greet(0, r)
        lax.fori_loop(ROOT + 1, frames, greet_line, 0)

    @pl.when(jnp.logical_not(is_root))
    def _():
        to_root(0).start()

    def to_others(i, carry):
        to_root(i).start()
        return carry

    lax.fori_loop(rows // 2, rows, to_others, 0)
    lax.fori_loop(1, rows // 2, to_others, 0)

    fetch = pltpu.make_async_copy(weight, raw, in_sem.at[0])
    fetch.start()
    gains = pltpu.make_async_copy(gain, scale, in_sem.at[1])
    gains.start()

    down = pltpu.make_async_remote_copy(
        src_ref=held.at[1:3, 96:144], dst_ref=held.at[1:3, 0:48], send_sem=halo_send.at[0],
        recv_sem=halo_recv.at[0], device_id=(f, below), device_id_type=MESH,
    )
    up = pltpu.make_async_remote_copy(
        src_ref=held.at[1:3, 48:96], dst_ref=held.at[1:3, 144:192], send_sem=halo_send.at[1],
        recv_sem=halo_recv.at[1], device_id=(f, above), device_id_type=MESH,
    )

    @pl.when(jnp.logical_not(below_later))
    def _():
        down.start()

    @pl.when(jnp.logical_not(above_later))
    def _():
        up.start()

    fetch.wait()
    gains.wait()

    def fold(step, carry):
        at = pl.multiple_of(step * 16, 16)
        for half in range(2):
            lanes = slice(128 * half, 128 * half + 128)
            for kind in range(3):
                def tap(h, w):
                    if kind == 0:
                        return raw[h * 3 + w, pl.ds(at, 16), lanes].astype(F32) + raw[
                            9 + h * 3 + w, pl.ds(at, 16), lanes].astype(F32)
                    return raw[(18 if kind == 1 else 9) + h * 3 + w, pl.ds(at, 16), lanes].astype(F32)

                t = [[tap(h, w) for w in range(3)] for h in range(3)]
                by_row = [[t[0], [t[1][w] + t[2][w] for w in range(3)]],
                          [[t[0][w] + t[1][w] for w in range(3)], t[2]]]
                for p in range(2):
                    for a in range(2):
                        u = by_row[p][a]
                        by_col = [[u[0], u[1] + u[2]], [u[0] + u[1], u[2]]]
                        for q in range(2):
                            for b in range(2):
                                base = kind * 1024 + (a * 2 + b) * 256
                                folded[p * 2 + q, pl.ds(base + at, 16), lanes] = by_col[q][b].astype(BF16)
        return carry

    lax.fori_loop(0, 16, fold, 0)

    @pl.when(below_later)
    def _():
        up.wait_recv()
        down.start()

    @pl.when(above_later)
    def _():
        down.wait_recv()
        up.start()

    @pl.when(jnp.logical_not(below_later))
    def _():
        up.wait_recv()

    @pl.when(jnp.logical_not(above_later))
    def _():
        down.wait_recv()

    forward = pltpu.make_async_remote_copy(
        src_ref=held.at[2], dst_ref=held.at[0], send_sem=halo_send.at[2], recv_sem=halo_recv.at[2],
        device_id=((f + 1) % frames, r), device_id_type=MESH,
    )

    def arrived(k):
        pltpu.make_async_copy(buf1.at[k], buf1.at[k], recv1.at[k]).wait()

    def pass_on():
        @pl.when(f + 1 < frames)
        def _():
            forward.start()

        @pl.when(f > 0)
        def _():
            forward.wait_recv()

        @pl.when(f == 0)
        def _():
            held[0] = held[1]

        halo_out[...] = held[...]

    others = buf1.at[ROOT, 0:rows - 1]
    heard = final.at[0:frames - 1]

    @pl.when(is_root)
    def _():
        def gather(k):
            lines[k] = merged(buf1[k], 192.0 * GROUP)

        def tell(k):
            pl.semaphore_signal(ready, inc=1, device_id=(k - 1, r), device_id_type=MESH)

        pltpu.make_async_copy(others, others, recv1.at[ROOT]).wait()
        gather(ROOT)
        for k in (0, ROOT + 1):
            arrived(k)
            gather(k)
        pass_on()

        def collect(k, carry):
            arrived(k)
            tell(k)
            gather(k)
            return carry

        def collect_late(k, carry):
            arrived(k)
            tell(k)
            return carry

        lax.fori_loop(ROOT + 2, frames - LATE, collect, 0)
        lax.fori_loop(frames - LATE, frames, collect_late, 0)
        for k in range(frames - LATE, frames):
            gather(k)
        final[0] = merged(lines[...], 192.0 * GROUP * rows)

        def send_third(k, carry):
            pltpu.make_async_remote_copy(
                src_ref=final.at[0], dst_ref=final.at[0], send_sem=send3, recv_sem=recv3,
                device_id=(k, r), device_id_type=MESH,
            ).start()
            return carry

        send_third(0, 0)
        lax.fori_loop(ROOT + 1, frames, send_third, 0)

    @pl.when(jnp.logical_not(is_root))
    def _():
        @pl.when((f > ROOT) & (f + 1 < frames))
        def _():
            pl.semaphore_wait(ready, 1)

        pass_on()
        pltpu.make_async_copy(final.at[0], final.at[0], recv3).wait()

    line = jnp.broadcast_to(final[0], (8, 128))
    kind = lane_index((8, 128)) & 7
    spread = []
    for k in range(4):
        v = jnp.where(kind == k, line, 0.0)
        for distance in (1, 2, 4):
            v = v + swapped(v, distance)
        spread.append(v[0:1])
    var = jnp.concatenate(spread[2:], axis=1) * (1.0 / total)
    stat_out[0:1] = jnp.concatenate(spread[:2], axis=1)
    stat_out[1:2] = lax.rsqrt(var + 1e-06) * scale[...]

    @pl.when(jnp.logical_not(is_root))
    def _():
        pltpu.make_async_copy(buf1.at[0], buf1.at[0], send1).wait()

    @pl.when(is_root)
    def _():
        pltpu.make_async_copy(others, others, send1).wait()
        pltpu.make_async_copy(heard, heard, send3).wait()

    down.wait_send()
    up.wait_send()

    @pl.when(f + 1 < frames)
    def _():
        forward.wait_send()


def conv_kernel(shape, halo, stat, folded, out, act, even_rows, odd_rows, wide, staged, out_sem):
    rows = shape
    r = lax.axis_index("row")

    mean, scale = stat[0:1], stat[1:2]
    for t in range(3):
        v = (halo[t, :, :].astype(F32)[24:168] - mean) * scale
        v = (v / (1.0 + jnp.exp(-v))).astype(BF16).astype(F32).reshape(6, 24, 256)
        top = jnp.where(r == 0, v[1:2], v[0:1])
        bottom = jnp.where(r == rows - 1, v[4:5], v[5:6])
        v = jnp.concatenate([top, v[1:5], bottom], axis=0)
        act[t, :, 8:32, :] = v
        act[t, :, 7:8, :] = v[:, 0:1]
        act[t, :, 32:33, :] = v[:, 23:24]
    for s in range(3):
        v = [act[t, :, 7 + s:31 + s, :] for t in range(3)]
        v = v + [v[1] - v[0], v[2] - v[1]]
        for t in range(5):
            even_rows[s, t] = v[t].reshape(144, 256).astype(BF16)
            odd_rows[s, t] = v[t][1:5].reshape(96, 256).astype(BF16)

    def piece(kind, sr, sc):
        first = (0, 1, 3)[kind]
        if sr == 1:
            return odd_rows[sc, first:first + 2].reshape(192, 256)
        return even_rows[sc, first:first + 2, 24 * sr:24 * sr + 96].reshape(192, 256)

    copies = []
    for p in range(2):
        for q in range(2):
            def taps(kind):
                return [piece(kind, p + a, q + b) for a in range(2) for b in range(2)]

            first = jnp.dot(jnp.concatenate(taps(0) + taps(1), axis=1), folded[p * 2 + q, 0:2048],
                            preferred_element_type=F32)
            step = jnp.dot(jnp.concatenate(taps(2), axis=1), folded[p * 2 + q, 2048:3072],
                           preferred_element_type=F32)
            second = first + step
            for i in range(2):
                for alpha, v in enumerate((first, second)):
                    for half in range(2):
                        lanes = slice(128 * half, 128 * half + 128)
                        wide[half, 2 * i + alpha, :, pl.ds(q, 24, 2), :] = v[96 * i:96 * i + 96, lanes].reshape(
                            4, 24, 128)
        for half in range(2):
            staged[p, :, :, :, 128 * half:128 * half + 128] = wide[half].astype(BF16)
        copy = pltpu.make_async_copy(staged.at[p], out.at[:, :, p], out_sem.at[p])
        copy.start()
        copies.append(copy)
    for copy in copies:
        copy.wait()


def solution(mesh):
    frames, rows = mesh.shape["frame"], mesh.shape["row"]
    xdim = 4 if rows % 4 == 0 else 1
    any_, vmem = pl.BlockSpec(memory_space=pltpu.HBM), pl.BlockSpec(memory_space=pltpu.VMEM)

    def shards(features, norm_gain, conv_up):
        voxels = float(192 * GROUP * frames * rows)
        halo, stat, folded = pl.pallas_call(
            functools.partial(comm_kernel, (frames, rows // xdim, xdim, voxels)),
            out_shape=(pltpu.VMEM((3, 192, 256), BF16), pltpu.VMEM((2, 256), F32), pltpu.VMEM((4, 3072, 256), BF16)),
            in_specs=[any_, any_, any_],
            out_specs=(vmem, vmem, vmem),
            scratch_shapes=[
                pltpu.VMEM((27, 256, 256), BF16),
                pltpu.VMEM((3, 192, 256), BF16),
                pltpu.VMEM((1, 256), F32),
                pltpu.VMEM((1, 128), F32),
                pltpu.VMEM((frames, rows, 1, 128), F32),
                pltpu.VMEM((frames, 1, 128), F32),
                pltpu.VMEM((frames - 1, 1, 128), F32),
                pltpu.SemaphoreType.DMA((6,)),
                pltpu.SemaphoreType.DMA,
                pltpu.SemaphoreType.DMA((frames,)),
                pltpu.SemaphoreType.DMA,
                pltpu.SemaphoreType.DMA,
                pltpu.SemaphoreType.DMA((3,)),
                pltpu.SemaphoreType.DMA((3,)),
                pltpu.SemaphoreType.REGULAR,
            ],
            compiler_params=pltpu.CompilerParams(
                collective_id=0, has_side_effects=True, vmem_limit_bytes=54 * 2**20),
            name="statistics",
        )(features.reshape(2, 96, 256), conv_up.reshape(27, 256, 256), norm_gain.reshape(1, 256))
        out = pl.pallas_call(
            functools.partial(conv_kernel, rows),
            out_shape=jax.ShapeDtypeStruct((4, 4, 2, 48, 256), BF16),
            in_specs=[vmem, vmem, vmem],
            out_specs=any_,
            scratch_shapes=[
                pltpu.VMEM((3, 6, 40, 256), F32),
                pltpu.VMEM((3, 5, 144, 256), BF16),
                pltpu.VMEM((3, 5, 96, 256), BF16),
                pltpu.VMEM((2, 4, 4, 48, 128), F32),
                pltpu.VMEM((2, 4, 4, 48, 256), BF16),
                pltpu.SemaphoreType.DMA((2,)),
            ],
            compiler_params=pltpu.CompilerParams(vmem_limit_bytes=24 * 2**20),
            name="conv",
        )(halo, stat, folded)
        return out.reshape(4, 8, 48, 256)

    spec = P("frame", "row", None, None)
    return jax.shard_map(shards, mesh=mesh, in_specs=(spec, P(), P()), out_specs=spec, check_vma=False)
```

```python
import functools

import jax
import jax.numpy as jnp
from jax import lax
from jax.experimental import pallas as pl
from jax.experimental.pallas import tpu as pltpu
from jax.sharding import PartitionSpec as P

MESH = pl.DeviceIdType.MESH
GROUP = 8
F32, BF16 = jnp.float32, jnp.bfloat16
ROOT, AIDE = 1, 3
LATE = 6


def lane_index(shape):
    return lax.broadcasted_iota(jnp.int32, shape, len(shape) - 1)


def swapped(value, distance):
    upper = (lane_index(value.shape) & distance) == 0
    return jnp.where(upper, pltpu.roll(value, 128 - distance, 1), pltpu.roll(value, distance, 1))


def local_statistics(own, rows):
    count = float(rows)
    mean = jnp.sum(own, axis=0, keepdims=True) * (1.0 / count)
    spread = jnp.sum(jnp.square(own - mean), axis=0, keepdims=True)
    packed = jnp.zeros((8, 128), F32)
    kind = lane_index((8, 128)) & 7
    for half in range(2):
        lanes = slice(128 * half, 128 * half + 128)
        m = jnp.broadcast_to(mean[:, lanes], (8, 128))
        s = jnp.broadcast_to(spread[:, lanes], (8, 128))
        held = count
        for distance in (1, 2, 4):
            other_m, other_s = swapped(m, distance), swapped(s, distance)
            s = s + other_s + (0.5 * held) * jnp.square(m - other_m)
            m = 0.5 * (m + other_m)
            held *= 2.0
        packed = jnp.where(kind == half, m, jnp.where(kind == 2 + half, s, packed))
    return packed[0:1]


def comm_kernel(
    shape, feat, weight, gain, halo_out, stat_out, folded,
    raw, held, scale, msg1, buf1, final,
    in_sem, send1, recv1, send3, recv3, halo_send, halo_recv, ready,
):
    frames, ydim, xdim, total = shape
    rows = ydim * xdim
    f, r = lax.axis_index("frame"), lax.axis_index("row")
    y, x = r // xdim, r % xdim
    is_root = f == ROOT
    is_aide = (f == AIDE) & (r == 0)
    is_hub = is_root | is_aide
    passes_on = (is_root & (r > 0)) | is_aide

    loads = [
        pltpu.make_async_copy(feat.at[t, part], held.at[1 + t, pl.ds(48 + part.start, 48)], in_sem.at[2 + 2 * t + i])
        for t in range(2) for i, part in enumerate((slice(0, 48), slice(48, 96)))
    ]
    for load in loads:
        load.start()

    def order(row):
        return row % xdim * rows + row

    below, above = (r + 1) % rows, (r + rows - 1) % rows
    below_later, above_later = order(below) > order(r), order(above) > order(r)

    def plane(i):
        return ((y + i // xdim) % ydim) * xdim + (x + i) % xdim

    def share_to(frame, row):
        return pltpu.make_async_remote_copy(
            src_ref=msg1, dst_ref=buf1.at[f, r], send_sem=send1, recv_sem=recv1.at[f],
            device_id=(frame, row), device_id_type=MESH,
        )

    barrier = pltpu.get_barrier_semaphore()

    def greet(frame, row):
        pl.semaphore_signal(barrier, inc=1, device_id=(frame, row), device_id_type=MESH)

    def greet_plane(i, carry):
        greet(f, plane(i))
        return carry

    def greet_line(k, carry):
        greet(k, r)
        return carry

    @pl.when(is_root)
    def _():
        lax.fori_loop(1, rows, greet_plane, 0)

    @pl.when(jnp.logical_not(is_root))
    def _():
        @pl.when(below_later)
        def _():
            greet(f, below)

        @pl.when(above_later)
        def _():
            greet(f, above)

    @pl.when(is_aide)
    def _():
        def greet_root(k, carry):
            greet(ROOT, k)
            return carry

        lax.fori_loop(0, rows, greet_root, 0)

    for load in loads:
        load.wait()
    values = held[1:3, 48:144].astype(F32).reshape(192, 256)
    mine = local_statistics(values, 192)
    msg1[...] = mine
    pl.semaphore_wait(barrier, jnp.where(
        is_root, rows, 3 - below_later.astype(jnp.int32) - above_later.astype(jnp.int32)))

    @pl.when(is_root)
    def _():
        greet(0, r)
        lax.fori_loop(ROOT + 1, frames, greet_line, 0)

    @pl.when(is_hub)
    def _():
        buf1[f, r] = mine

    @pl.when(jnp.logical_not(is_root))
    def _():
        share_to(ROOT, r).start()

    def to_roots(i, carry):
        share_to(ROOT, plane(i)).start()
        return carry

    lax.fori_loop(rows // 2, rows, to_roots, 0)

    @pl.when(jnp.logical_not(is_aide))
    def _():
        share_to(AIDE, 0).start()

    lax.fori_loop(1, rows // 2, to_roots, 0)

    fetch = pltpu.make_async_copy(weight, raw, in_sem.at[0])
    fetch.start()
    gains = pltpu.make_async_copy(gain, scale, in_sem.at[1])
    gains.start()

    down = pltpu.make_async_remote_copy(
        src_ref=held.at[1:3, 96:144], dst_ref=held.at[1:3, 0:48], send_sem=halo_send.at[0],
        recv_sem=halo_recv.at[0], device_id=(f, below), device_id_type=MESH,
    )
    up = pltpu.make_async_remote_copy(
        src_ref=held.at[1:3, 48:96], dst_ref=held.at[1:3, 144:192], send_sem=halo_send.at[1],
        recv_sem=halo_recv.at[1], device_id=(f, above), device_id_type=MESH,
    )

    @pl.when(jnp.logical_not(below_later))
    def _():
        down.start()

    @pl.when(jnp.logical_not(above_later))
    def _():
        up.start()

    fetch.wait()
    gains.wait()

    def fold(step, carry):
        at = pl.multiple_of(step * 16, 16)
        for half in range(2):
            lanes = slice(128 * half, 128 * half + 128)
            for kind in range(3):
                def tap(h, w):
                    if kind == 0:
                        return raw[h * 3 + w, pl.ds(at, 16), lanes].astype(F32) + raw[
                            9 + h * 3 + w, pl.ds(at, 16), lanes].astype(F32)
                    return raw[(18 if kind == 1 else 9) + h * 3 + w, pl.ds(at, 16), lanes].astype(F32)

                t = [[tap(h, w) for w in range(3)] for h in range(3)]
                by_row = [[t[0], [t[1][w] + t[2][w] for w in range(3)]],
                          [[t[0][w] + t[1][w] for w in range(3)], t[2]]]
                for p in range(2):
                    for a in range(2):
                        u = by_row[p][a]
                        by_col = [[u[0], u[1] + u[2]], [u[0] + u[1], u[2]]]
                        for q in range(2):
                            for b in range(2):
                                base = kind * 1024 + (a * 2 + b) * 256
                                folded[p * 2 + q, pl.ds(base + at, 16), lanes] = by_col[q][b].astype(BF16)
        return carry

    lax.fori_loop(0, 16, fold, 0)

    @pl.when(below_later)
    def _():
        up.wait_recv()
        down.start()

    @pl.when(above_later)
    def _():
        down.wait_recv()
        up.start()

    @pl.when(jnp.logical_not(below_later))
    def _():
        up.wait_recv()

    @pl.when(jnp.logical_not(above_later))
    def _():
        down.wait_recv()

    forward = pltpu.make_async_remote_copy(
        src_ref=held.at[2], dst_ref=held.at[0], send_sem=halo_send.at[2], recv_sem=halo_recv.at[2],
        device_id=((f + 1) % frames, r), device_id_type=MESH,
    )

    def pass_on():
        @pl.when(f + 1 < frames)
        def _():
            forward.start()

        @pl.when(f > 0)
        def _():
            forward.wait_recv()

        @pl.when(f == 0)
        def _():
            held[0] = held[1]

        halo_out[...] = held[...]

    others = buf1.at[ROOT, 0:rows - 1]

    @pl.when(is_hub)
    def _():
        is_mean = (lane_index((1, 128)) & 7) < 2
        pivot = jnp.where(is_mean, mine, 0.0)

        def arrived(k):
            @pl.when(k != f)
            def _():
                pltpu.make_async_copy(buf1.at[k], buf1.at[k], recv1.at[k]).wait()

            @pl.when(k == f)
            def _():
                pltpu.make_async_copy(others, others, recv1.at[k]).wait()

            @pl.when(is_root & (k > ROOT + 1))
            def _():
                pl.semaphore_signal(ready, inc=1, device_id=(k - 1, r), device_id_type=MESH)

        def gather(k, sums):
            shares = buf1[k] - pivot[None]
            return sums[0] + jnp.sum(shares, axis=0), sums[1] + jnp.sum(jnp.square(shares), axis=0)

        def collect(k, sums):
            arrived(k)
            return gather(k, sums)

        sums = (jnp.zeros((1, 128), F32), jnp.zeros((1, 128), F32))
        sums = lax.fori_loop(0, ROOT + 2, collect, sums)

        @pl.when(is_root)
        def _():
            pass_on()

        sums = lax.fori_loop(ROOT + 2, frames - LATE, collect, sums)

        @pl.when(is_aide)
        def _():
            pl.semaphore_wait(ready, 1)
            pass_on()

        for k in range(frames - LATE, frames):
            arrived(k)
        for k in range(frames - LATE, frames):
            sums = gather(k, sums)
        share = sums[0] * (1.0 / (frames * rows))
        apart = jnp.broadcast_to(sums[1] - sums[0] * share, (8, 128))
        final[0] = jnp.where(is_mean, pivot + share, sums[0] + 192.0 * GROUP * pltpu.roll(apart, 2, 1)[0:1])

    @pl.when(passes_on)
    def _():
        def send_third(k, carry):
            @pl.when((k != ROOT) & (k != f))
            def _():
                pltpu.make_async_remote_copy(
                    src_ref=final.at[0], dst_ref=final.at[0], send_sem=send3, recv_sem=recv3,
                    device_id=(k, r), device_id_type=MESH,
                ).start()

            return carry

        lax.fori_loop(0, frames, send_third, 0)

    @pl.when(jnp.logical_not(is_hub))
    def _():
        @pl.when((f > ROOT) & (f + 1 < frames))
        def _():
            pl.semaphore_wait(ready, 1)

        pass_on()
        pltpu.make_async_copy(final.at[0], final.at[0], recv3).wait()

    line = jnp.broadcast_to(final[0], (8, 128))
    kind = lane_index((8, 128)) & 7
    spread = []
    for k in range(4):
        v = jnp.where(kind == k, line, 0.0)
        for distance in (1, 2, 4):
            v = v + swapped(v, distance)
        spread.append(v[0:1])
    var = jnp.concatenate(spread[2:], axis=1) * (1.0 / total)
    stat_out[0:1] = jnp.concatenate(spread[:2], axis=1)
    stat_out[1:2] = lax.rsqrt(var + 1e-06) * scale[...]

    @pl.when(jnp.logical_not(is_hub))
    def _():
        everyone = buf1.at[0, 0:1]
        pltpu.make_async_copy(everyone, everyone, send1).wait()

    every_root = buf1.at[0]
    pltpu.make_async_copy(every_root, every_root, send1).wait()

    @pl.when(passes_on)
    def _():
        heard = final.at[0:frames - 2]
        pltpu.make_async_copy(heard, heard, send3).wait()

    @pl.when(passes_on & is_root)
    def _():
        pltpu.make_async_copy(final.at[0], final.at[0], send3).wait()

    down.wait_send()
    up.wait_send()

    @pl.when(f + 1 < frames)
    def _():
        forward.wait_send()


def conv_kernel(shape, halo, stat, folded, out, act, even_rows, odd_rows, wide, staged, out_sem):
    rows = shape
    r = lax.axis_index("row")

    mean, scale = stat[0:1], stat[1:2]
    for t in range(3):
        v = (halo[t, :, :].astype(F32)[24:168] - mean) * scale
        v = (v / (1.0 + jnp.exp(-v))).astype(BF16).astype(F32).reshape(6, 24, 256)
        top = jnp.where(r == 0, v[1:2], v[0:1])
        bottom = jnp.where(r == rows - 1, v[4:5], v[5:6])
        v = jnp.concatenate([top, v[1:5], bottom], axis=0)
        act[t, :, 8:32, :] = v
        act[t, :, 7:8, :] = v[:, 0:1]
        act[t, :, 32:33, :] = v[:, 23:24]
    for s in range(3):
        v = [act[t, :, 7 + s:31 + s, :] for t in range(3)]
        v = v + [v[1] - v[0], v[2] - v[1]]
        for t in range(5):
            even_rows[s, t] = v[t].reshape(144, 256).astype(BF16)
            odd_rows[s, t] = v[t][1:5].reshape(96, 256).astype(BF16)

    def piece(kind, sr, sc):
        first = (0, 1, 3)[kind]
        if sr == 1:
            return odd_rows[sc, first:first + 2].reshape(192, 256)
        return even_rows[sc, first:first + 2, 24 * sr:24 * sr + 96].reshape(192, 256)

    copies = []
    for p in range(2):
        for q in range(2):
            def taps(kind):
                return [piece(kind, p + a, q + b) for a in range(2) for b in range(2)]

            first = jnp.dot(jnp.concatenate(taps(0) + taps(1), axis=1), folded[p * 2 + q, 0:2048],
                            preferred_element_type=F32)
            step = jnp.dot(jnp.concatenate(taps(2), axis=1), folded[p * 2 + q, 2048:3072],
                           preferred_element_type=F32)
            second = first + step
            for i in range(2):
                for alpha, v in enumerate((first, second)):
                    for half in range(2):
                        lanes = slice(128 * half, 128 * half + 128)
                        wide[half, 2 * i + alpha, :, pl.ds(q, 24, 2), :] = v[96 * i:96 * i + 96, lanes].reshape(
                            4, 24, 128)
        for half in range(2):
            staged[p, :, :, :, 128 * half:128 * half + 128] = wide[half].astype(BF16)
        copy = pltpu.make_async_copy(staged.at[p], out.at[:, :, p], out_sem.at[p])
        copy.start()
        copies.append(copy)
    for copy in copies:
        copy.wait()


def solution(mesh):
    frames, rows = mesh.shape["frame"], mesh.shape["row"]
    xdim = 4 if rows % 4 == 0 else 1
    any_, vmem = pl.BlockSpec(memory_space=pltpu.HBM), pl.BlockSpec(memory_space=pltpu.VMEM)

    def shards(features, norm_gain, conv_up):
        voxels = float(192 * GROUP * frames * rows)
        halo, stat, folded = pl.pallas_call(
            functools.partial(comm_kernel, (frames, rows // xdim, xdim, voxels)),
            out_shape=(pltpu.VMEM((3, 192, 256), BF16), pltpu.VMEM((2, 256), F32), pltpu.VMEM((4, 3072, 256), BF16)),
            in_specs=[any_, any_, any_],
            out_specs=(vmem, vmem, vmem),
            scratch_shapes=[
                pltpu.VMEM((27, 256, 256), BF16),
                pltpu.VMEM((3, 192, 256), BF16),
                pltpu.VMEM((1, 256), F32),
                pltpu.VMEM((1, 128), F32),
                pltpu.VMEM((frames, rows, 1, 128), F32),
                pltpu.VMEM((frames - 1, 1, 128), F32),
                pltpu.SemaphoreType.DMA((6,)),
                pltpu.SemaphoreType.DMA,
                pltpu.SemaphoreType.DMA((frames,)),
                pltpu.SemaphoreType.DMA,
                pltpu.SemaphoreType.DMA,
                pltpu.SemaphoreType.DMA((3,)),
                pltpu.SemaphoreType.DMA((3,)),
                pltpu.SemaphoreType.REGULAR,
            ],
            compiler_params=pltpu.CompilerParams(
                collective_id=0, has_side_effects=True, vmem_limit_bytes=54 * 2**20),
            name="statistics",
        )(features.reshape(2, 96, 256), conv_up.reshape(27, 256, 256), norm_gain.reshape(1, 256))
        out = pl.pallas_call(
            functools.partial(conv_kernel, rows),
            out_shape=jax.ShapeDtypeStruct((4, 4, 2, 48, 256), BF16),
            in_specs=[vmem, vmem, vmem],
            out_specs=any_,
            scratch_shapes=[
                pltpu.VMEM((3, 6, 40, 256), F32),
                pltpu.VMEM((3, 5, 144, 256), BF16),
                pltpu.VMEM((3, 5, 96, 256), BF16),
                pltpu.VMEM((2, 4, 4, 48, 128), F32),
                pltpu.VMEM((2, 4, 4, 48, 256), BF16),
                pltpu.SemaphoreType.DMA((2,)),
            ],
            compiler_params=pltpu.CompilerParams(vmem_limit_bytes=24 * 2**20),
            name="conv",
        )(halo, stat, folded)
        return out.reshape(4, 8, 48, 256)

    spec = P("frame", "row", None, None)
    return jax.shard_map(shards, mesh=mesh, in_specs=(spec, P(), P()), out_specs=spec, check_vma=False)
```

```python
import functools

import jax
import jax.numpy as jnp
from jax import lax
from jax.experimental import pallas as pl
from jax.experimental.pallas import tpu as pltpu
from jax.sharding import PartitionSpec as P

MESH = pl.DeviceIdType.MESH
GROUP = 8
F32, BF16 = jnp.float32, jnp.bfloat16
ROOT, AIDE = 1, 3
LATE = 6


def lane_index(shape):
    return lax.broadcasted_iota(jnp.int32, shape, len(shape) - 1)


def swapped(value, distance):
    upper = (lane_index(value.shape) & distance) == 0
    return jnp.where(upper, pltpu.roll(value, 128 - distance, 1), pltpu.roll(value, distance, 1))


def local_statistics(own, rows):
    count = float(rows)
    pivot = own[0:1]
    apart = own - pivot
    offset = jnp.sum(apart, axis=0, keepdims=True)
    spread = jnp.sum(jnp.square(apart), axis=0, keepdims=True) - offset * offset * (1.0 / count)
    mean = pivot + offset * (1.0 / count)
    packed = jnp.zeros((8, 128), F32)
    kind = lane_index((8, 128)) & 3
    for half in range(2):
        lanes = slice(128 * half, 128 * half + 128)
        m = jnp.broadcast_to(mean[:, lanes], (8, 128))
        s = jnp.broadcast_to(spread[:, lanes], (8, 128))
        held = count
        for distance in (1, 2, 4):
            other_m, other_s = swapped(m, distance), swapped(s, distance)
            s = s + other_s + (0.5 * held) * jnp.square(m - other_m)
            m = 0.5 * (m + other_m)
            held *= 2.0
        packed = jnp.where(kind == half, m, jnp.where(kind == 2 + half, s, packed))
    return packed[0:1]


def comm_kernel(
    shape, feat, weight, gain, halo_out, stat_out, folded,
    raw, held, scale, msg1, buf1, final,
    in_sem, send1, recv1, send3, recv3, halo_send, halo_recv, ready,
):
    frames, ydim, xdim, total = shape
    rows = ydim * xdim
    f, r = lax.axis_index("frame"), lax.axis_index("row")
    y, x = r // xdim, r % xdim
    is_root = f == ROOT
    is_aide = (f == AIDE) & (r == 0)
    is_hub = is_root | is_aide
    passes_on = (is_root & (r > 0)) | is_aide

    loads = [
        pltpu.make_async_copy(feat.at[t, part], held.at[1 + t, pl.ds(48 + part.start, 48)], in_sem.at[2 + 2 * t + i])
        for t in range(2) for i, part in enumerate((slice(0, 48), slice(48, 96)))
    ]
    for load in loads:
        load.start()

    def order(row):
        return row % xdim * rows + row

    below, above = (r + 1) % rows, (r + rows - 1) % rows
    below_later, above_later = order(below) > order(r), order(above) > order(r)

    def plane(i):
        return ((y + i // xdim) % ydim) * xdim + (x + i) % xdim

    def share_to(frame, row):
        return pltpu.make_async_remote_copy(
            src_ref=msg1, dst_ref=buf1.at[f, pl.ds(r, 1)], send_sem=send1, recv_sem=recv1.at[f],
            device_id=(frame, row), device_id_type=MESH,
        )

    barrier = pltpu.get_barrier_semaphore()

    def greet(frame, row):
        pl.semaphore_signal(barrier, inc=1, device_id=(frame, row), device_id_type=MESH)

    def greet_plane(i, carry):
        greet(f, plane(i))
        return carry

    def greet_line(k, carry):
        greet(k, r)
        return carry

    @pl.when(is_root)
    def _():
        lax.fori_loop(1, rows, greet_plane, 0)

    @pl.when(jnp.logical_not(is_root))
    def _():
        @pl.when(below_later)
        def _():
            greet(f, below)

        @pl.when(above_later)
        def _():
            greet(f, above)

    @pl.when(is_aide)
    def _():
        def greet_root(k, carry):
            greet(ROOT, k)
            return carry

        lax.fori_loop(0, rows, greet_root, 0)

    for load in loads:
        load.wait()
    values = held[1:3, 48:144].astype(F32).reshape(192, 256)
    mine = local_statistics(values, 192)
    msg1[...] = mine
    pl.semaphore_wait(barrier, jnp.where(
        is_root, rows, 3 - below_later.astype(jnp.int32) - above_later.astype(jnp.int32)))

    @pl.when(is_root)
    def _():
        greet(0, r)
        lax.fori_loop(ROOT + 1, frames, greet_line, 0)

    @pl.when(is_hub)
    def _():
        buf1[f, pl.ds(r, 1)] = mine

    @pl.when(jnp.logical_not(is_root))
    def _():
        share_to(ROOT, r).start()

    def to_roots(i, carry):
        share_to(ROOT, plane(i)).start()
        return carry

    lax.fori_loop(rows // 2, rows, to_roots, 0)

    @pl.when(jnp.logical_not(is_aide))
    def _():
        share_to(AIDE, 0).start()

    lax.fori_loop(1, rows // 2, to_roots, 0)

    fetch = pltpu.make_async_copy(weight, raw, in_sem.at[0])
    fetch.start()
    gains = pltpu.make_async_copy(gain, scale, in_sem.at[1])
    gains.start()

    down = pltpu.make_async_remote_copy(
        src_ref=held.at[1:3, 96:144], dst_ref=held.at[1:3, 0:48], send_sem=halo_send.at[0],
        recv_sem=halo_recv.at[0], device_id=(f, below), device_id_type=MESH,
    )
    up = pltpu.make_async_remote_copy(
        src_ref=held.at[1:3, 48:96], dst_ref=held.at[1:3, 144:192], send_sem=halo_send.at[1],
        recv_sem=halo_recv.at[1], device_id=(f, above), device_id_type=MESH,
    )

    @pl.when(jnp.logical_not(below_later))
    def _():
        down.start()

    @pl.when(jnp.logical_not(above_later))
    def _():
        up.start()

    fetch.wait()
    gains.wait()

    def fold(step, carry):
        at = pl.multiple_of(step * 16, 16)
        for half in range(2):
            lanes = slice(128 * half, 128 * half + 128)
            for kind in range(3):
                def tap(h, w):
                    if kind == 0:
                        return raw[h * 3 + w, pl.ds(at, 16), lanes].astype(F32) + raw[
                            9 + h * 3 + w, pl.ds(at, 16), lanes].astype(F32)
                    return raw[(18 if kind == 1 else 9) + h * 3 + w, pl.ds(at, 16), lanes].astype(F32)

                t = [[tap(h, w) for w in range(3)] for h in range(3)]
                by_row = [[t[0], [t[1][w] + t[2][w] for w in range(3)]],
                          [[t[0][w] + t[1][w] for w in range(3)], t[2]]]
                for p in range(2):
                    for a in range(2):
                        u = by_row[p][a]
                        by_col = [[u[0], u[1] + u[2]], [u[0] + u[1], u[2]]]
                        for q in range(2):
                            for b in range(2):
                                base = kind * 1024 + (a * 2 + b) * 256
                                folded[p * 2 + q, pl.ds(base + at, 16), lanes] = by_col[q][b].astype(BF16)
        return carry

    lax.fori_loop(0, 16, fold, 0)

    @pl.when(below_later)
    def _():
        up.wait_recv()
        down.start()

    @pl.when(above_later)
    def _():
        down.wait_recv()
        up.start()

    @pl.when(jnp.logical_not(below_later))
    def _():
        up.wait_recv()

    @pl.when(jnp.logical_not(above_later))
    def _():
        down.wait_recv()

    forward = pltpu.make_async_remote_copy(
        src_ref=held.at[2], dst_ref=held.at[0], send_sem=halo_send.at[2], recv_sem=halo_recv.at[2],
        device_id=((f + 1) % frames, r), device_id_type=MESH,
    )

    def pass_on():
        @pl.when(f + 1 < frames)
        def _():
            forward.start()

        @pl.when(f > 0)
        def _():
            forward.wait_recv()

        @pl.when(f == 0)
        def _():
            held[0] = held[1]

        halo_out[...] = held[...]

    others = buf1.at[ROOT, 0:rows - 1]

    @pl.when(is_hub)
    def _():
        is_mean = (lane_index((1, 128)) & 3) < 2
        pivot = jnp.where(is_mean, mine, 0.0)

        def arrived(k):
            @pl.when(k != f)
            def _():
                pltpu.make_async_copy(buf1.at[k], buf1.at[k], recv1.at[k]).wait()

            @pl.when(k == f)
            def _():
                pltpu.make_async_copy(others, others, recv1.at[k]).wait()

            @pl.when(is_root & (k > ROOT + 1))
            def _():
                pl.semaphore_signal(ready, inc=1, device_id=(k - 1, r), device_id_type=MESH)

        def gather(k, sums):
            shares = (buf1[k] - pivot).reshape(rows // 8, 8, 128)
            return sums[0] + jnp.sum(shares, axis=0), sums[1] + jnp.sum(jnp.square(shares), axis=0)

        def collect(k, sums):
            arrived(k)
            return gather(k, sums)

        sums = (jnp.zeros((8, 128), F32), jnp.zeros((8, 128), F32))
        sums = lax.fori_loop(0, ROOT + 2, collect, sums)

        @pl.when(is_root)
        def _():
            pass_on()

        sums = lax.fori_loop(ROOT + 2, frames - LATE, collect, sums)

        @pl.when(is_aide)
        def _():
            pl.semaphore_wait(ready, 1)
            pass_on()

        for k in range(frames - LATE, frames):
            arrived(k)
        for k in range(frames - LATE, frames):
            sums = gather(k, sums)
        offset = jnp.sum(sums[0], axis=0, keepdims=True)
        share = offset * (1.0 / (frames * rows))
        apart = jnp.broadcast_to(jnp.sum(sums[1], axis=0, keepdims=True) - offset * share, (8, 128))
        final[0] = jnp.where(is_mean, pivot + share, offset + 192.0 * GROUP * pltpu.roll(apart, 2, 1)[0:1])

    @pl.when(passes_on)
    def _():
        def send_third(k, carry):
            @pl.when((k != ROOT) & (k != f))
            def _():
                pltpu.make_async_remote_copy(
                    src_ref=final.at[0], dst_ref=final.at[0], send_sem=send3, recv_sem=recv3,
                    device_id=(k, r), device_id_type=MESH,
                ).start()

            return carry

        lax.fori_loop(0, frames, send_third, 0)

    @pl.when(jnp.logical_not(is_hub))
    def _():
        @pl.when((f > ROOT) & (f + 1 < frames))
        def _():
            pl.semaphore_wait(ready, 1)

        pass_on()
        pltpu.make_async_copy(final.at[0], final.at[0], recv3).wait()

    line = jnp.broadcast_to(final[0], (8, 128))
    kind = lane_index((8, 128)) & 3
    by_one = swapped(line, 1)
    near = (line, by_one, swapped(line, 2), swapped(by_one, 2))
    spread = []
    for k in range(4):
        v = near[0]
        for distance in range(1, 4):
            v = jnp.where((kind ^ k) == distance, near[distance], v)
        spread.append(v[0:1])
    var = jnp.concatenate(spread[2:], axis=1) * (1.0 / total)
    stat_out[0:1] = jnp.concatenate(spread[:2], axis=1)
    stat_out[1:2] = lax.rsqrt(var + 1e-06) * scale[...]

    @pl.when(jnp.logical_not(is_hub))
    def _():
        everyone = buf1.at[0, 0:1]
        pltpu.make_async_copy(everyone, everyone, send1).wait()

    every_root = buf1.at[0]
    pltpu.make_async_copy(every_root, every_root, send1).wait()

    @pl.when(passes_on)
    def _():
        heard = final.at[0:frames - 2]
        pltpu.make_async_copy(heard, heard, send3).wait()

    @pl.when(passes_on & is_root)
    def _():
        pltpu.make_async_copy(final.at[0], final.at[0], send3).wait()

    down.wait_send()
    up.wait_send()

    @pl.when(f + 1 < frames)
    def _():
        forward.wait_send()


def conv_kernel(shape, halo, stat, folded, out, act, even_rows, odd_rows, wide, staged, out_sem):
    rows = shape
    r = lax.axis_index("row")

    mean, scale = stat[0:1], stat[1:2]
    for t in range(3):
        v = (halo[t, :, :].astype(F32)[24:168] - mean) * scale
        v = (v / (1.0 + jnp.exp(-v))).astype(BF16).astype(F32).reshape(6, 24, 256)
        top = jnp.where(r == 0, v[1:2], v[0:1])
        bottom = jnp.where(r == rows - 1, v[4:5], v[5:6])
        v = jnp.concatenate([top, v[1:5], bottom], axis=0)
        act[t, :, 8:32, :] = v
        act[t, :, 7:8, :] = v[:, 0:1]
        act[t, :, 32:33, :] = v[:, 23:24]
    for s in range(3):
        v = [act[t, :, 7 + s:31 + s, :] for t in range(3)]
        v = v + [v[1] - v[0], v[2] - v[1]]
        for t in range(5):
            even_rows[s, t] = v[t].reshape(144, 256).astype(BF16)
            odd_rows[s, t] = v[t][1:5].reshape(96, 256).astype(BF16)

    def piece(kind, sr, sc):
        first = (0, 1, 3)[kind]
        if sr == 1:
            return odd_rows[sc, first:first + 2].reshape(192, 256)
        return even_rows[sc, first:first + 2, 24 * sr:24 * sr + 96].reshape(192, 256)

    copies = []
    for p in range(2):
        for q in range(2):
            def taps(kind):
                return [piece(kind, p + a, q + b) for a in range(2) for b in range(2)]

            first = jnp.dot(jnp.concatenate(taps(0) + taps(1), axis=1), folded[p * 2 + q, 0:2048],
                            preferred_element_type=F32)
            step = jnp.dot(jnp.concatenate(taps(2), axis=1), folded[p * 2 + q, 2048:3072],
                           preferred_element_type=F32)
            second = first + step
            for i in range(2):
                for alpha, v in enumerate((first, second)):
                    for half in range(2):
                        lanes = slice(128 * half, 128 * half + 128)
                        wide[half, 2 * i + alpha, :, pl.ds(q, 24, 2), :] = v[96 * i:96 * i + 96, lanes].reshape(
                            4, 24, 128)
        for half in range(2):
            staged[p, :, :, :, 128 * half:128 * half + 128] = wide[half].astype(BF16)
        copy = pltpu.make_async_copy(staged.at[p], out.at[:, :, p], out_sem.at[p])
        copy.start()
        copies.append(copy)
    for copy in copies:
        copy.wait()


def solution(mesh):
    frames, rows = mesh.shape["frame"], mesh.shape["row"]
    xdim = 4 if rows % 4 == 0 else 1
    any_, vmem = pl.BlockSpec(memory_space=pltpu.HBM), pl.BlockSpec(memory_space=pltpu.VMEM)

    def shards(features, norm_gain, conv_up):
        voxels = float(192 * GROUP * frames * rows)
        halo, stat, folded = pl.pallas_call(
            functools.partial(comm_kernel, (frames, rows // xdim, xdim, voxels)),
            out_shape=(pltpu.VMEM((3, 192, 256), BF16), pltpu.VMEM((2, 256), F32), pltpu.VMEM((4, 3072, 256), BF16)),
            in_specs=[any_, any_, any_],
            out_specs=(vmem, vmem, vmem),
            scratch_shapes=[
                pltpu.VMEM((27, 256, 256), BF16),
                pltpu.VMEM((3, 192, 256), BF16),
                pltpu.VMEM((1, 256), F32),
                pltpu.VMEM((1, 128), F32),
                pltpu.VMEM((frames, rows, 128), F32),
                pltpu.VMEM((frames - 1, 1, 128), F32),
                pltpu.SemaphoreType.DMA((6,)),
                pltpu.SemaphoreType.DMA,
                pltpu.SemaphoreType.DMA((frames,)),
                pltpu.SemaphoreType.DMA,
                pltpu.SemaphoreType.DMA,
                pltpu.SemaphoreType.DMA((3,)),
                pltpu.SemaphoreType.DMA((3,)),
                pltpu.SemaphoreType.REGULAR,
            ],
            compiler_params=pltpu.CompilerParams(
                collective_id=0, has_side_effects=True, vmem_limit_bytes=54 * 2**20),
            name="statistics",
        )(features.reshape(2, 96, 256), conv_up.reshape(27, 256, 256), norm_gain.reshape(1, 256))
        out = pl.pallas_call(
            functools.partial(conv_kernel, rows),
            out_shape=jax.ShapeDtypeStruct((4, 4, 2, 48, 256), BF16),
            in_specs=[vmem, vmem, vmem],
            out_specs=any_,
            scratch_shapes=[
                pltpu.VMEM((3, 6, 40, 256), F32),
                pltpu.VMEM((3, 5, 144, 256), BF16),
                pltpu.VMEM((3, 5, 96, 256), BF16),
                pltpu.VMEM((2, 4, 4, 48, 128), F32),
                pltpu.VMEM((2, 4, 4, 48, 256), BF16),
                pltpu.SemaphoreType.DMA((2,)),
            ],
            compiler_params=pltpu.CompilerParams(vmem_limit_bytes=24 * 2**20),
            name="conv",
        )(halo, stat, folded)
        return out.reshape(4, 8, 48, 256)

    spec = P("frame", "row", None, None)
    return jax.shard_map(shards, mesh=mesh, in_specs=(spec, P(), P()), out_specs=spec, check_vma=False)
```

```python
import functools

import jax
import jax.numpy as jnp
from jax import lax
from jax.experimental import pallas as pl
from jax.experimental.pallas import tpu as pltpu
from jax.sharding import PartitionSpec as P

MESH = pl.DeviceIdType.MESH
GROUP = 8
F32, BF16 = jnp.float32, jnp.bfloat16
ROOT, AIDE = 1, 3
LATE = 6


def lane_index(shape):
    return lax.broadcasted_iota(jnp.int32, shape, len(shape) - 1)


def swapped(value, distance):
    upper = (lane_index(value.shape) & distance) == 0
    return jnp.where(upper, pltpu.roll(value, 128 - distance, 1), pltpu.roll(value, distance, 1))


def local_statistics(own, rows):
    count = float(rows)
    pivot = own[0:1]
    apart = own - pivot
    offset = jnp.sum(apart, axis=0, keepdims=True)
    spread = jnp.sum(jnp.square(apart), axis=0, keepdims=True) - offset * offset * (1.0 / count)
    mean = pivot + offset * (1.0 / count)
    packed = jnp.zeros((8, 128), F32)
    kind = lane_index((8, 128)) & 3
    for half in range(2):
        lanes = slice(128 * half, 128 * half + 128)
        m = jnp.broadcast_to(mean[:, lanes], (8, 128))
        s = jnp.broadcast_to(spread[:, lanes], (8, 128))
        held = count
        for distance in (1, 2, 4):
            other_m, other_s = swapped(m, distance), swapped(s, distance)
            s = s + other_s + (0.5 * held) * jnp.square(m - other_m)
            m = 0.5 * (m + other_m)
            held *= 2.0
        packed = jnp.where(kind == half, m, jnp.where(kind == 2 + half, s, packed))
    return packed[0:1]


def comm_kernel(
    shape, feat, weight, gain, halo_out, stat_out, folded,
    raw, held, scale, msg1, buf1, final,
    in_sem, send1, recv1, send3, recv3, halo_send, halo_recv, ready,
):
    frames, ydim, xdim, total = shape
    rows = ydim * xdim
    f, r = lax.axis_index("frame"), lax.axis_index("row")
    y, x = r // xdim, r % xdim
    is_root = f == ROOT
    is_aide = (f == AIDE) & (r == 0)
    is_hub = is_root | is_aide
    passes_on = (is_root & (r > 0)) | is_aide

    loads = [
        pltpu.make_async_copy(feat.at[t, part], held.at[1 + t, pl.ds(48 + part.start, 48)], in_sem.at[2 + 2 * t + i])
        for t in range(2) for i, part in enumerate((slice(0, 48), slice(48, 96)))
    ]
    for load in loads:
        load.start()

    def order(row):
        return row % xdim * rows + row

    below, above = (r + 1) % rows, (r + rows - 1) % rows
    below_later, above_later = order(below) > order(r), order(above) > order(r)

    def plane(i):
        return ((y + i // xdim) % ydim) * xdim + (x + i) % xdim

    def share_to(frame, row):
        return pltpu.make_async_remote_copy(
            src_ref=msg1, dst_ref=buf1.at[f, pl.ds(r, 1)], send_sem=send1, recv_sem=recv1.at[f],
            device_id=(frame, row), device_id_type=MESH,
        )

    barrier = pltpu.get_barrier_semaphore()

    def greet(frame, row):
        pl.semaphore_signal(barrier, inc=1, device_id=(frame, row), device_id_type=MESH)

    def greet_plane(i, carry):
        greet(f, plane(i))
        return carry

    def greet_line(k, carry):
        greet(k, r)
        return carry

    @pl.when(is_root)
    def _():
        lax.fori_loop(1, rows, greet_plane, 0)

    @pl.when(jnp.logical_not(is_root))
    def _():
        @pl.when(below_later)
        def _():
            greet(f, below)

        @pl.when(above_later)
        def _():
            greet(f, above)

    @pl.when(is_aide)
    def _():
        def greet_root(k, carry):
            greet(ROOT, k)
            return carry

        lax.fori_loop(0, rows, greet_root, 0)

    for load in loads:
        load.wait()
    values = held[1:3, 48:144].astype(F32).reshape(192, 256)
    mine = local_statistics(values, 192)
    msg1[...] = mine
    pl.semaphore_wait(barrier, jnp.where(
        is_root, rows, 3 - below_later.astype(jnp.int32) - above_later.astype(jnp.int32)))

    @pl.when(is_root)
    def _():
        greet(0, r)
        lax.fori_loop(ROOT + 1, frames, greet_line, 0)

    @pl.when(is_hub)
    def _():
        buf1[f, pl.ds(r, 1)] = mine

    @pl.when(jnp.logical_not(is_root))
    def _():
        share_to(ROOT, r).start()

    def to_roots(i, carry):
        share_to(ROOT, plane(i)).start()
        return carry

    lax.fori_loop(rows // 2, rows, to_roots, 0)

    @pl.when(jnp.logical_not(is_aide))
    def _():
        share_to(AIDE, 0).start()

    lax.fori_loop(1, rows // 2, to_roots, 0)

    fetch = pltpu.make_async_copy(weight, raw, in_sem.at[0])
    fetch.start()
    gains = pltpu.make_async_copy(gain, scale, in_sem.at[1])
    gains.start()

    down = pltpu.make_async_remote_copy(
        src_ref=held.at[1:3, 96:144], dst_ref=held.at[1:3, 0:48], send_sem=halo_send.at[0],
        recv_sem=halo_recv.at[0], device_id=(f, below), device_id_type=MESH,
    )
    up = pltpu.make_async_remote_copy(
        src_ref=held.at[1:3, 48:96], dst_ref=held.at[1:3, 144:192], send_sem=halo_send.at[1],
        recv_sem=halo_recv.at[1], device_id=(f, above), device_id_type=MESH,
    )

    @pl.when(jnp.logical_not(below_later))
    def _():
        down.start()

    @pl.when(jnp.logical_not(above_later))
    def _():
        up.start()

    fetch.wait()
    gains.wait()

    def fold(step, carry):
        at = pl.multiple_of(step * 16, 16)
        for half in range(2):
            lanes = slice(128 * half, 128 * half + 128)
            for kind in range(3):
                def tap(h, w):
                    if kind == 0:
                        return raw[h * 3 + w, pl.ds(at, 16), lanes].astype(F32) + raw[
                            9 + h * 3 + w, pl.ds(at, 16), lanes].astype(F32)
                    return raw[(18 if kind == 1 else 9) + h * 3 + w, pl.ds(at, 16), lanes].astype(F32)

                t = [[tap(h, w) for w in range(3)] for h in range(3)]
                by_row = [[t[0], [t[1][w] + t[2][w] for w in range(3)]],
                          [[t[0][w] + t[1][w] for w in range(3)], t[2]]]
                for p in range(2):
                    for a in range(2):
                        u = by_row[p][a]
                        by_col = [[u[0], u[1] + u[2]], [u[0] + u[1], u[2]]]
                        for q in range(2):
                            for b in range(2):
                                base = kind * 1024 + (a * 2 + b) * 256
                                folded[p * 2 + q, pl.ds(base + at, 16), lanes] = by_col[q][b].astype(BF16)
        return carry

    lax.fori_loop(0, 16, fold, 0)

    @pl.when(below_later)
    def _():
        up.wait_recv()
        down.start()

    @pl.when(above_later)
    def _():
        down.wait_recv()
        up.start()

    @pl.when(jnp.logical_not(below_later))
    def _():
        up.wait_recv()

    @pl.when(jnp.logical_not(above_later))
    def _():
        down.wait_recv()

    forward = pltpu.make_async_remote_copy(
        src_ref=held.at[2], dst_ref=held.at[0], send_sem=halo_send.at[2], recv_sem=halo_recv.at[2],
        device_id=((f + 1) % frames, r), device_id_type=MESH,
    )

    def pass_on():
        @pl.when(f + 1 < frames)
        def _():
            forward.start()

        @pl.when(f > 0)
        def _():
            forward.wait_recv()

        @pl.when(f == 0)
        def _():
            held[0] = held[1]

        halo_out[...] = held[...]

    others = buf1.at[ROOT, 0:rows - 1]

    @pl.when(is_hub)
    def _():
        is_mean = (lane_index((1, 128)) & 3) < 2
        pivot = jnp.where(is_mean, mine, 0.0)

        def arrived(k):
            @pl.when(k != f)
            def _():
                pltpu.make_async_copy(buf1.at[k], buf1.at[k], recv1.at[k]).wait()

            @pl.when(k == f)
            def _():
                pltpu.make_async_copy(others, others, recv1.at[k]).wait()

            @pl.when(is_root & (k > ROOT + 1))
            def _():
                pl.semaphore_signal(ready, inc=1, device_id=(k - 1, r), device_id_type=MESH)

        def collect(k, carry):
            arrived(k)
            return carry

        lax.fori_loop(0, ROOT + 2, collect, 0)

        @pl.when(is_root)
        def _():
            pass_on()

        lax.fori_loop(ROOT + 2, frames - LATE, collect, 0)

        @pl.when(is_aide)
        def _():
            pl.semaphore_wait(ready, 1)
            pass_on()

        for k in range(frames - LATE, frames):
            arrived(k)
        shares = (buf1[...] - pivot).reshape(frames * rows // 8, 8, 128)
        sums = jnp.sum(shares, axis=0), jnp.sum(jnp.square(shares), axis=0)
        offset = jnp.sum(sums[0], axis=0, keepdims=True)
        share = offset * (1.0 / (frames * rows))
        apart = jnp.broadcast_to(jnp.sum(sums[1], axis=0, keepdims=True) - offset * share, (8, 128))
        final[0] = jnp.where(is_mean, pivot + share, offset + 192.0 * GROUP * pltpu.roll(apart, 2, 1)[0:1])

    @pl.when(passes_on)
    def _():
        def send_third(k, carry):
            @pl.when((k != ROOT) & (k != f))
            def _():
                pltpu.make_async_remote_copy(
                    src_ref=final.at[0], dst_ref=final.at[0], send_sem=send3, recv_sem=recv3,
                    device_id=(k, r), device_id_type=MESH,
                ).start()

            return carry

        lax.fori_loop(0, frames, send_third, 0)

    @pl.when(jnp.logical_not(is_hub))
    def _():
        @pl.when((f > ROOT) & (f + 1 < frames))
        def _():
            pl.semaphore_wait(ready, 1)

        pass_on()
        pltpu.make_async_copy(final.at[0], final.at[0], recv3).wait()

    line = jnp.broadcast_to(final[0], (8, 128))
    kind = lane_index((8, 128)) & 3
    by_one = swapped(line, 1)
    near = (line, by_one, swapped(line, 2), swapped(by_one, 2))
    spread = []
    for k in range(4):
        v = near[0]
        for distance in range(1, 4):
            v = jnp.where((kind ^ k) == distance, near[distance], v)
        spread.append(v[0:1])
    var = jnp.concatenate(spread[2:], axis=1) * (1.0 / total)
    stat_out[0:1] = jnp.concatenate(spread[:2], axis=1)
    stat_out[1:2] = lax.rsqrt(var + 1e-06) * scale[...]

    @pl.when(jnp.logical_not(is_hub))
    def _():
        everyone = buf1.at[0, 0:1]
        pltpu.make_async_copy(everyone, everyone, send1).wait()

    every_root = buf1.at[0]
    pltpu.make_async_copy(every_root, every_root, send1).wait()

    @pl.when(passes_on)
    def _():
        heard = final.at[0:frames - 2]
        pltpu.make_async_copy(heard, heard, send3).wait()

    @pl.when(passes_on & is_root)
    def _():
        pltpu.make_async_copy(final.at[0], final.at[0], send3).wait()

    down.wait_send()
    up.wait_send()

    @pl.when(f + 1 < frames)
    def _():
        forward.wait_send()


def conv_kernel(shape, halo, stat, folded, out, act, even_rows, odd_rows, wide, staged, out_sem):
    rows = shape
    r = lax.axis_index("row")

    mean, scale = stat[0:1], stat[1:2]
    for t in range(3):
        v = (halo[t, :, :].astype(F32)[24:168] - mean) * scale
        v = (v / (1.0 + jnp.exp(-v))).astype(BF16).astype(F32).reshape(6, 24, 256)
        top = jnp.where(r == 0, v[1:2], v[0:1])
        bottom = jnp.where(r == rows - 1, v[4:5], v[5:6])
        v = jnp.concatenate([top, v[1:5], bottom], axis=0)
        act[t, :, 8:32, :] = v
        act[t, :, 7:8, :] = v[:, 0:1]
        act[t, :, 32:33, :] = v[:, 23:24]
    for s in range(3):
        v = [act[t, :, 7 + s:31 + s, :] for t in range(3)]
        v = v + [v[1] - v[0], v[2] - v[1]]
        for t in range(5):
            even_rows[s, t] = v[t].reshape(144, 256).astype(BF16)
            odd_rows[s, t] = v[t][1:5].reshape(96, 256).astype(BF16)

    def piece(kind, sr, sc):
        first = (0, 1, 3)[kind]
        if sr == 1:
            return odd_rows[sc, first:first + 2].reshape(192, 256)
        return even_rows[sc, first:first + 2, 24 * sr:24 * sr + 96].reshape(192, 256)

    copies = []
    for p in range(2):
        for q in range(2):
            def product(kinds):
                total = None
                for kind in kinds:
                    for a in range(2):
                        for b in range(2):
                            at = kind * 1024 + (a * 2 + b) * 256
                            term = jnp.dot(piece(kind, p + a, q + b), folded[p * 2 + q, at:at + 256],
                                           preferred_element_type=F32)
                            total = term if total is None else total + term
                return total

            first, step = product((0, 1)), product((2,))
            second = first + step
            for i in range(2):
                for alpha, v in enumerate((first, second)):
                    for half in range(2):
                        lanes = slice(128 * half, 128 * half + 128)
                        wide[half, 2 * i + alpha, :, pl.ds(q, 24, 2), :] = v[96 * i:96 * i + 96, lanes].reshape(
                            4, 24, 128)
        size = 4 if p == 0 else 1
        for at in range(0, 4, size):
            part = slice(at, at + size)
            for half in range(2):
                lanes = slice(128 * half, 128 * half + 128)
                staged[p, part, :, :, lanes] = wide[half, part, :, 0:48].astype(BF16)
            copy = pltpu.make_async_copy(staged.at[p, part], out.at[part, :, p], out_sem.at[p, at])
            copy.start()
            copies.append(copy)
    for copy in copies:
        copy.wait()


def solution(mesh):
    frames, rows = mesh.shape["frame"], mesh.shape["row"]
    xdim = 4 if rows % 4 == 0 else 1
    any_, vmem = pl.BlockSpec(memory_space=pltpu.HBM), pl.BlockSpec(memory_space=pltpu.VMEM)

    def shards(features, norm_gain, conv_up):
        voxels = float(192 * GROUP * frames * rows)
        halo, stat, folded = pl.pallas_call(
            functools.partial(comm_kernel, (frames, rows // xdim, xdim, voxels)),
            out_shape=(pltpu.VMEM((3, 192, 256), BF16), pltpu.VMEM((2, 256), F32), pltpu.VMEM((4, 3072, 256), BF16)),
            in_specs=[any_, any_, any_],
            out_specs=(vmem, vmem, vmem),
            scratch_shapes=[
                pltpu.VMEM((27, 256, 256), BF16),
                pltpu.VMEM((3, 192, 256), BF16),
                pltpu.VMEM((1, 256), F32),
                pltpu.VMEM((1, 128), F32),
                pltpu.VMEM((frames, rows, 128), F32),
                pltpu.VMEM((frames - 1, 1, 128), F32),
                pltpu.SemaphoreType.DMA((6,)),
                pltpu.SemaphoreType.DMA,
                pltpu.SemaphoreType.DMA((frames,)),
                pltpu.SemaphoreType.DMA,
                pltpu.SemaphoreType.DMA,
                pltpu.SemaphoreType.DMA((3,)),
                pltpu.SemaphoreType.DMA((3,)),
                pltpu.SemaphoreType.REGULAR,
            ],
            compiler_params=pltpu.CompilerParams(
                collective_id=0, has_side_effects=True, vmem_limit_bytes=54 * 2**20),
            name="statistics",
        )(features.reshape(2, 96, 256), conv_up.reshape(27, 256, 256), norm_gain.reshape(1, 256))
        out = pl.pallas_call(
            functools.partial(conv_kernel, rows),
            out_shape=jax.ShapeDtypeStruct((4, 4, 2, 48, 256), BF16),
            in_specs=[vmem, vmem, vmem],
            out_specs=any_,
            scratch_shapes=[
                pltpu.VMEM((3, 6, 40, 256), F32),
                pltpu.VMEM((3, 5, 144, 256), BF16),
                pltpu.VMEM((3, 5, 96, 256), BF16),
                pltpu.VMEM((2, 4, 4, 56, 128), F32),
                pltpu.VMEM((2, 4, 4, 48, 256), BF16),
                pltpu.SemaphoreType.DMA((2, 4)),
            ],
            compiler_params=pltpu.CompilerParams(vmem_limit_bytes=24 * 2**20),
            name="conv",
        )(halo, stat, folded)
        return out.reshape(4, 8, 48, 256)

    spec = P("frame", "row", None, None)
    return jax.shard_map(shards, mesh=mesh, in_specs=(spec, P(), P()), out_specs=spec, check_vma=False)
```

```python
import functools

import jax
import jax.numpy as jnp
from jax import lax
from jax.experimental import pallas as pl
from jax.experimental.pallas import tpu as pltpu
from jax.sharding import PartitionSpec as P

MESH = pl.DeviceIdType.MESH
GROUP = 8
F32, BF16 = jnp.float32, jnp.bfloat16
ROOT, AIDE = 1, 3
LATE = 6


def lane_index(shape):
    return lax.broadcasted_iota(jnp.int32, shape, len(shape) - 1)


def swapped(value, distance):
    upper = (lane_index(value.shape) & distance) == 0
    return jnp.where(upper, pltpu.roll(value, 128 - distance, 1), pltpu.roll(value, distance, 1))


def quad(value):
    lane = lane_index(value.shape) & 3
    after = [pltpu.roll(value, 128 - d, 1) for d in (1, 2, 3)]
    before = [pltpu.roll(value, d, 1) for d in (1, 2, 3)]
    one = jnp.where((lane & 1) == 0, after[0], before[0])
    two = jnp.where(lane < 2, after[1], before[1])
    three = jnp.where(lane == 0, after[2], jnp.where(lane == 3, before[2], jnp.where(lane == 1, after[0], before[0])))
    return value, one, two, three


def local_statistics(own, rows):
    count = float(rows)
    pivot = own[0:1]
    apart = own - pivot
    offset = jnp.sum(apart, axis=0, keepdims=True)
    spread = jnp.sum(jnp.square(apart), axis=0, keepdims=True) - offset * offset * (1.0 / count)
    mean = pivot + offset * (1.0 / count)
    low = lax.broadcasted_iota(jnp.int32, (8, 128), 0) == 0

    def halves(v):
        return jnp.where(low, jnp.broadcast_to(v[:, 0:128], (8, 128)), jnp.broadcast_to(v[:, 128:256], (8, 128)))

    means, spreads = quad(halves(mean)), quad(halves(spread))
    m = 0.25 * ((means[0] + means[1]) + (means[2] + means[3]))
    s = (spreads[0] + spreads[1]) + (spreads[2] + spreads[3])
    s = s + count * sum(jnp.square(v - m) for v in means)
    other_m, other_s = swapped(m, 4), swapped(s, 4)
    s = s + other_s + (2.0 * count) * jnp.square(m - other_m)
    m = 0.5 * (m + other_m)
    kind = lane_index((1, 128)) & 3
    return jnp.where(kind == 0, m[0:1], jnp.where(kind == 1, m[1:2], jnp.where(kind == 2, s[0:1], s[1:2])))


def comm_kernel(
    shape, feat, weight, gain, halo_out, stat_out, folded,
    raw, held, scale, msg1, buf1, final,
    in_sem, send1, recv1, send3, recv3, halo_send, halo_recv, ready,
):
    frames, ydim, xdim, total = shape
    rows = ydim * xdim
    f, r = lax.axis_index("frame"), lax.axis_index("row")
    y, x = r // xdim, r % xdim
    is_root = f == ROOT
    is_aide = (f == AIDE) & (r == 0)
    is_hub = is_root | is_aide
    passes_on = (is_root & (r > 0)) | is_aide

    loads = [
        pltpu.make_async_copy(feat.at[t, part], held.at[1 + t, pl.ds(48 + part.start, 48)], in_sem.at[2 + 2 * t + i])
        for t in range(2) for i, part in enumerate((slice(0, 48), slice(48, 96)))
    ]
    for load in loads:
        load.start()

    def order(row):
        return row % xdim * rows + row

    below, above = (r + 1) % rows, (r + rows - 1) % rows
    below_later, above_later = order(below) > order(r), order(above) > order(r)

    def plane(i):
        return ((y + i // xdim) % ydim) * xdim + (x + i) % xdim

    def share_to(frame, row):
        return pltpu.make_async_remote_copy(
            src_ref=msg1, dst_ref=buf1.at[f, pl.ds(r, 1)], send_sem=send1, recv_sem=recv1.at[f],
            device_id=(frame, row), device_id_type=MESH,
        )

    barrier = pltpu.get_barrier_semaphore()

    def greet(frame, row):
        pl.semaphore_signal(barrier, inc=1, device_id=(frame, row), device_id_type=MESH)

    def greet_plane(i, carry):
        greet(f, plane(i))
        return carry

    def greet_line(k, carry):
        greet(k, r)
        return carry

    @pl.when(is_root)
    def _():
        lax.fori_loop(1, rows, greet_plane, 0)

    @pl.when(jnp.logical_not(is_root))
    def _():
        @pl.when(below_later)
        def _():
            greet(f, below)

        @pl.when(above_later)
        def _():
            greet(f, above)

    @pl.when(is_aide)
    def _():
        def greet_root(k, carry):
            greet(ROOT, k)
            return carry

        lax.fori_loop(0, rows, greet_root, 0)

    for load in loads:
        load.wait()
    values = held[1:3, 48:144].astype(F32).reshape(192, 256)
    mine = local_statistics(values, 192)
    msg1[...] = mine
    pl.semaphore_wait(barrier, jnp.where(
        is_root, rows, 3 - below_later.astype(jnp.int32) - above_later.astype(jnp.int32)))

    @pl.when(is_root)
    def _():
        greet(0, r)
        lax.fori_loop(ROOT + 1, frames, greet_line, 0)

    @pl.when(is_hub)
    def _():
        buf1[f, pl.ds(r, 1)] = mine

    @pl.when(jnp.logical_not(is_root))
    def _():
        share_to(ROOT, r).start()

    def to_roots(i, carry):
        share_to(ROOT, plane(i)).start()
        return carry

    lax.fori_loop(rows // 2, rows, to_roots, 0)

    @pl.when(jnp.logical_not(is_aide))
    def _():
        share_to(AIDE, 0).start()

    lax.fori_loop(1, rows // 2, to_roots, 0)

    fetch = pltpu.make_async_copy(weight, raw, in_sem.at[0])
    fetch.start()
    gains = pltpu.make_async_copy(gain, scale, in_sem.at[1])
    gains.start()

    down = pltpu.make_async_remote_copy(
        src_ref=held.at[1:3, 96:144], dst_ref=held.at[1:3, 0:48], send_sem=halo_send.at[0],
        recv_sem=halo_recv.at[0], device_id=(f, below), device_id_type=MESH,
    )
    up = pltpu.make_async_remote_copy(
        src_ref=held.at[1:3, 48:96], dst_ref=held.at[1:3, 144:192], send_sem=halo_send.at[1],
        recv_sem=halo_recv.at[1], device_id=(f, above), device_id_type=MESH,
    )

    @pl.when(jnp.logical_not(below_later))
    def _():
        down.start()

    @pl.when(jnp.logical_not(above_later))
    def _():
        up.start()

    fetch.wait()
    gains.wait()

    def fold(step, carry):
        at = pl.multiple_of(step * 16, 16)
        for half in range(2):
            lanes = slice(128 * half, 128 * half + 128)
            for kind in range(3):
                def tap(h, w):
                    if kind == 0:
                        return raw[h * 3 + w, pl.ds(at, 16), lanes].astype(F32) + raw[
                            9 + h * 3 + w, pl.ds(at, 16), lanes].astype(F32)
                    return raw[(18 if kind == 1 else 9) + h * 3 + w, pl.ds(at, 16), lanes].astype(F32)

                t = [[tap(h, w) for w in range(3)] for h in range(3)]
                by_row = [[t[0], [t[1][w] + t[2][w] for w in range(3)]],
                          [[t[0][w] + t[1][w] for w in range(3)], t[2]]]
                for p in range(2):
                    for a in range(2):
                        u = by_row[p][a]
                        by_col = [[u[0], u[1] + u[2]], [u[0] + u[1], u[2]]]
                        for q in range(2):
                            for b in range(2):
                                base = kind * 1024 + (a * 2 + b) * 256
                                folded[p * 2 + q, pl.ds(base + at, 16), lanes] = by_col[q][b].astype(BF16)
        return carry

    lax.fori_loop(0, 16, fold, 0)

    @pl.when(below_later)
    def _():
        up.wait_recv()
        down.start()

    @pl.when(above_later)
    def _():
        down.wait_recv()
        up.start()

    @pl.when(jnp.logical_not(below_later))
    def _():
        up.wait_recv()

    @pl.when(jnp.logical_not(above_later))
    def _():
        down.wait_recv()

    forward = pltpu.make_async_remote_copy(
        src_ref=held.at[2], dst_ref=held.at[0], send_sem=halo_send.at[2], recv_sem=halo_recv.at[2],
        device_id=((f + 1) % frames, r), device_id_type=MESH,
    )

    def pass_on():
        @pl.when(f + 1 < frames)
        def _():
            forward.start()

        @pl.when(f > 0)
        def _():
            forward.wait_recv()

        @pl.when(f == 0)
        def _():
            held[0] = held[1]

        halo_out[...] = held[...]

    others = buf1.at[ROOT, 0:rows - 1]

    @pl.when(is_hub)
    def _():
        is_mean = (lane_index((1, 128)) & 3) < 2
        pivot = jnp.where(is_mean, mine, 0.0)

        def arrived(k):
            @pl.when(k != f)
            def _():
                pltpu.make_async_copy(buf1.at[k], buf1.at[k], recv1.at[k]).wait()

            @pl.when(k == f)
            def _():
                pltpu.make_async_copy(others, others, recv1.at[k]).wait()

            @pl.when(is_root & (k > ROOT + 1))
            def _():
                pl.semaphore_signal(ready, inc=1, device_id=(k - 1, r), device_id_type=MESH)

        def collect(k, carry):
            arrived(k)
            return carry

        lax.fori_loop(0, ROOT + 2, collect, 0)

        @pl.when(is_root)
        def _():
            pass_on()

        lax.fori_loop(ROOT + 2, frames - LATE, collect, 0)

        @pl.when(is_aide)
        def _():
            pl.semaphore_wait(ready, 1)
            pass_on()

        for k in range(frames - LATE, frames):
            arrived(k)
        shares = (buf1[...] - pivot).reshape(frames * rows // 8, 8, 128)
        sums = jnp.sum(shares, axis=0), jnp.sum(jnp.square(shares), axis=0)
        offset = jnp.sum(sums[0], axis=0, keepdims=True)
        share = offset * (1.0 / (frames * rows))
        final[0, 0:1] = jnp.where(is_mean, pivot + share, offset)
        final[0, 1:2] = jnp.sum(sums[1], axis=0, keepdims=True) - offset * share

    @pl.when(passes_on)
    def _():
        def send_third(k, carry):
            @pl.when((k != ROOT) & (k != f))
            def _():
                pltpu.make_async_remote_copy(
                    src_ref=final.at[0], dst_ref=final.at[0], send_sem=send3, recv_sem=recv3,
                    device_id=(k, r), device_id_type=MESH,
                ).start()

            return carry

        lax.fori_loop(0, frames, send_third, 0)

    @pl.when(jnp.logical_not(is_hub))
    def _():
        @pl.when((f > ROOT) & (f + 1 < frames))
        def _():
            pl.semaphore_wait(ready, 1)

        pass_on()
        pltpu.make_async_copy(final.at[0], final.at[0], recv3).wait()

    kind = lane_index((8, 128)) & 3
    line, apart = (quad(jnp.broadcast_to(final[0, i:i + 1], (8, 128))) for i in range(2))

    def everywhere(near, k):
        v = near[0]
        for distance in range(1, 4):
            v = jnp.where((kind ^ k) == distance, near[distance], v)
        return v[0:1]

    spread = [everywhere(line, 0), everywhere(line, 1)]
    spread += [everywhere(line, 2 + h) + 192.0 * GROUP * everywhere(apart, h) for h in range(2)]
    var = jnp.concatenate(spread[2:], axis=1) * (1.0 / total)
    stat_out[0:1] = jnp.concatenate(spread[:2], axis=1)
    stat_out[1:2] = lax.rsqrt(var + 1e-06) * scale[...]

    @pl.when(jnp.logical_not(is_hub))
    def _():
        everyone = buf1.at[0, 0:1]
        pltpu.make_async_copy(everyone, everyone, send1).wait()

    every_root = buf1.at[0]
    pltpu.make_async_copy(every_root, every_root, send1).wait()

    @pl.when(passes_on)
    def _():
        heard = final.at[0:frames - 2]
        pltpu.make_async_copy(heard, heard, send3).wait()

    @pl.when(passes_on & is_root)
    def _():
        pltpu.make_async_copy(final.at[0], final.at[0], send3).wait()

    down.wait_send()
    up.wait_send()

    @pl.when(f + 1 < frames)
    def _():
        forward.wait_send()


def conv_kernel(shape, halo, stat, folded, out, act, even_rows, odd_rows, wide, staged, out_sem):
    rows = shape
    r = lax.axis_index("row")

    mean, scale = stat[0:1], stat[1:2]
    for t in range(3):
        v = (halo[t, :, :].astype(F32)[24:168] - mean) * scale
        v = (v / (1.0 + jnp.exp(-v))).astype(BF16).astype(F32).reshape(6, 24, 256)
        top = jnp.where(r == 0, v[1:2], v[0:1])
        bottom = jnp.where(r == rows - 1, v[4:5], v[5:6])
        v = jnp.concatenate([top, v[1:5], bottom], axis=0)
        act[t, :, 8:32, :] = v
        act[t, :, 7:8, :] = v[:, 0:1]
        act[t, :, 32:33, :] = v[:, 23:24]
    for s in range(3):
        v = [act[t, :, 7 + s:31 + s, :] for t in range(3)]
        v = v + [v[1] - v[0], v[2] - v[1]]
        for t in range(5):
            even_rows[s, t] = v[t].reshape(144, 256).astype(BF16)
            odd_rows[s, t] = v[t][1:5].reshape(96, 256).astype(BF16)

    def piece(kind, sr, sc):
        first = (0, 1, 3)[kind]
        if sr == 1:
            return odd_rows[sc, first:first + 2].reshape(192, 256)
        return even_rows[sc, first:first + 2, 24 * sr:24 * sr + 96].reshape(192, 256)

    copies = []
    for p in range(2):
        for q in range(2):
            def product(kinds):
                total = None
                for kind in kinds:
                    for a in range(2):
                        for b in range(2):
                            at = kind * 1024 + (a * 2 + b) * 256
                            term = jnp.dot(piece(kind, p + a, q + b), folded[p * 2 + q, at:at + 256],
                                           preferred_element_type=F32)
                            total = term if total is None else total + term
                return total

            first, step = product((0, 1)), product((2,))
            second = first + step
            for i in range(2):
                for alpha, v in enumerate((first, second)):
                    for half in range(2):
                        lanes = slice(128 * half, 128 * half + 128)
                        wide[half, 2 * i + alpha, :, pl.ds(q, 24, 2), :] = v[96 * i:96 * i + 96, lanes].reshape(
                            4, 24, 128)
        size = 4 if p == 0 else 1
        for at in range(0, 4, size):
            part = slice(at, at + size)
            for half in range(2):
                lanes = slice(128 * half, 128 * half + 128)
                staged[p, part, :, :, lanes] = wide[half, part, :, 0:48].astype(BF16)
            copy = pltpu.make_async_copy(staged.at[p, part], out.at[part, :, p], out_sem.at[p, at])
            copy.start()
            copies.append(copy)
    for copy in copies:
        copy.wait()


def solution(mesh):
    frames, rows = mesh.shape["frame"], mesh.shape["row"]
    xdim = 4 if rows % 4 == 0 else 1
    any_, vmem = pl.BlockSpec(memory_space=pltpu.HBM), pl.BlockSpec(memory_space=pltpu.VMEM)

    def shards(features, norm_gain, conv_up):
        voxels = float(192 * GROUP * frames * rows)
        halo, stat, folded = pl.pallas_call(
            functools.partial(comm_kernel, (frames, rows // xdim, xdim, voxels)),
            out_shape=(pltpu.VMEM((3, 192, 256), BF16), pltpu.VMEM((2, 256), F32), pltpu.VMEM((4, 3072, 256), BF16)),
            in_specs=[any_, any_, any_],
            out_specs=(vmem, vmem, vmem),
            scratch_shapes=[
                pltpu.VMEM((27, 256, 256), BF16),
                pltpu.VMEM((3, 192, 256), BF16),
                pltpu.VMEM((1, 256), F32),
                pltpu.VMEM((1, 128), F32),
                pltpu.VMEM((frames, rows, 128), F32),
                pltpu.VMEM((frames - 1, 2, 128), F32),
                pltpu.SemaphoreType.DMA((6,)),
                pltpu.SemaphoreType.DMA,
                pltpu.SemaphoreType.DMA((frames,)),
                pltpu.SemaphoreType.DMA,
                pltpu.SemaphoreType.DMA,
                pltpu.SemaphoreType.DMA((3,)),
                pltpu.SemaphoreType.DMA((3,)),
                pltpu.SemaphoreType.REGULAR,
            ],
            compiler_params=pltpu.CompilerParams(
                collective_id=0, has_side_effects=True, vmem_limit_bytes=54 * 2**20),
            name="statistics",
        )(features.reshape(2, 96, 256), conv_up.reshape(27, 256, 256), norm_gain.reshape(1, 256))
        out = pl.pallas_call(
            functools.partial(conv_kernel, rows),
            out_shape=jax.ShapeDtypeStruct((4, 4, 2, 48, 256), BF16),
            in_specs=[vmem, vmem, vmem],
            out_specs=any_,
            scratch_shapes=[
                pltpu.VMEM((3, 6, 40, 256), F32),
                pltpu.VMEM((3, 5, 144, 256), BF16),
                pltpu.VMEM((3, 5, 96, 256), BF16),
                pltpu.VMEM((2, 4, 4, 56, 128), F32),
                pltpu.VMEM((2, 4, 4, 48, 256), BF16),
                pltpu.SemaphoreType.DMA((2, 4)),
            ],
            compiler_params=pltpu.CompilerParams(vmem_limit_bytes=24 * 2**20),
            name="conv",
        )(halo, stat, folded)
        return out.reshape(4, 8, 48, 256)

    spec = P("frame", "row", None, None)
    return jax.shard_map(shards, mesh=mesh, in_specs=(spec, P(), P()), out_specs=spec, check_vma=False)
```

```python
import functools

import jax
import jax.numpy as jnp
from jax import lax
from jax.experimental import pallas as pl
from jax.experimental.pallas import tpu as pltpu
from jax.sharding import PartitionSpec as P

MESH = pl.DeviceIdType.MESH
GROUP = 8
F32, BF16 = jnp.float32, jnp.bfloat16
ROOT, AIDE = 1, 3
LATE = 8


def lane_index(shape):
    return lax.broadcasted_iota(jnp.int32, shape, len(shape) - 1)


def swapped(value, distance):
    upper = (lane_index(value.shape) & distance) == 0
    return jnp.where(upper, pltpu.roll(value, 128 - distance, 1), pltpu.roll(value, distance, 1))


def quad(value):
    lane = lane_index(value.shape) & 3
    after = [pltpu.roll(value, 128 - d, 1) for d in (1, 2, 3)]
    before = [pltpu.roll(value, d, 1) for d in (1, 2, 3)]
    one = jnp.where((lane & 1) == 0, after[0], before[0])
    two = jnp.where(lane < 2, after[1], before[1])
    three = jnp.where(lane == 0, after[2], jnp.where(lane == 3, before[2], jnp.where(lane == 1, after[0], before[0])))
    return value, one, two, three


def local_statistics(own, rows):
    count = float(rows)
    pivot = own[0:1]
    apart = own - pivot
    offset = jnp.sum(apart, axis=0, keepdims=True)
    spread = jnp.sum(jnp.square(apart), axis=0, keepdims=True) - offset * offset * (1.0 / count)
    mean = pivot + offset * (1.0 / count)
    low = lax.broadcasted_iota(jnp.int32, (8, 128), 0) == 0

    def halves(v):
        return jnp.where(low, jnp.broadcast_to(v[:, 0:128], (8, 128)), jnp.broadcast_to(v[:, 128:256], (8, 128)))

    means, spreads = quad(halves(mean)), quad(halves(spread))
    m = 0.25 * ((means[0] + means[1]) + (means[2] + means[3]))
    s = (spreads[0] + spreads[1]) + (spreads[2] + spreads[3])
    s = s + count * sum(jnp.square(v - m) for v in means)
    other_m, other_s = swapped(m, 4), swapped(s, 4)
    s = s + other_s + (2.0 * count) * jnp.square(m - other_m)
    m = 0.5 * (m + other_m)
    kind = lane_index((1, 128)) & 3
    return jnp.where(kind == 0, m[0:1], jnp.where(kind == 1, m[1:2], jnp.where(kind == 2, s[0:1], s[1:2])))


def comm_kernel(
    shape, feat, weight, gain, halo_out, stat_out, folded,
    raw, held, scale, msg1, buf1, final,
    in_sem, send1, recv1, send3, recv3, halo_send, halo_recv, ready,
):
    frames, ydim, xdim, total = shape
    rows = ydim * xdim
    f, r = lax.axis_index("frame"), lax.axis_index("row")
    y, x = r // xdim, r % xdim
    is_root = f == ROOT
    is_aide = (f == AIDE) & (r == 0)
    is_hub = is_root | is_aide
    passes_on = (is_root & (r > 0)) | is_aide

    loads = [
        pltpu.make_async_copy(feat.at[t, part], held.at[1 + t, pl.ds(48 + part.start, 48)], in_sem.at[2 + 2 * t + i])
        for t in range(2) for i, part in enumerate((slice(0, 48), slice(48, 96)))
    ]
    for load in loads:
        load.start()

    def order(row):
        return row % xdim * rows + row

    below, above = (r + 1) % rows, (r + rows - 1) % rows
    below_later, above_later = order(below) > order(r), order(above) > order(r)

    def plane(i):
        return ((y + i // xdim) % ydim) * xdim + (x + i) % xdim

    def share_to(frame, row):
        return pltpu.make_async_remote_copy(
            src_ref=msg1, dst_ref=buf1.at[f, pl.ds(r, 1)], send_sem=send1, recv_sem=recv1.at[f],
            device_id=(frame, row), device_id_type=MESH,
        )

    barrier = pltpu.get_barrier_semaphore()

    def greet(frame, row):
        pl.semaphore_signal(barrier, inc=1, device_id=(frame, row), device_id_type=MESH)

    def greet_plane(i, carry):
        greet(f, plane(i))
        return carry

    def greet_line(k, carry):
        greet(k, r)
        return carry

    @pl.when(is_root)
    def _():
        lax.fori_loop(1, rows, greet_plane, 0)

    @pl.when(jnp.logical_not(is_root))
    def _():
        @pl.when(below_later)
        def _():
            greet(f, below)

        @pl.when(above_later)
        def _():
            greet(f, above)

    @pl.when(is_aide)
    def _():
        def greet_root(k, carry):
            greet(ROOT, k)
            return carry

        lax.fori_loop(0, rows, greet_root, 0)

    for load in loads:
        load.wait()
    values = held[1:3, 48:144].astype(F32).reshape(192, 256)
    mine = local_statistics(values, 192)
    msg1[...] = mine
    pl.semaphore_wait(barrier, jnp.where(
        is_root, rows, 3 - below_later.astype(jnp.int32) - above_later.astype(jnp.int32)))

    @pl.when(is_root)
    def _():
        greet(0, r)
        lax.fori_loop(ROOT + 1, frames, greet_line, 0)

    @pl.when(is_hub)
    def _():
        buf1[f, pl.ds(r, 1)] = mine

    @pl.when(jnp.logical_not(is_root))
    def _():
        share_to(ROOT, r).start()

    def to_roots(i, carry):
        share_to(ROOT, plane(i)).start()
        return carry

    lax.fori_loop(rows // 2, rows, to_roots, 0)

    @pl.when(jnp.logical_not(is_aide))
    def _():
        share_to(AIDE, 0).start()

    lax.fori_loop(1, rows // 2, to_roots, 0)

    fetch = pltpu.make_async_copy(weight, raw, in_sem.at[0])
    fetch.start()
    gains = pltpu.make_async_copy(gain, scale, in_sem.at[1])
    gains.start()

    down = pltpu.make_async_remote_copy(
        src_ref=held.at[1:3, 96:144], dst_ref=held.at[1:3, 0:48], send_sem=halo_send.at[0],
        recv_sem=halo_recv.at[0], device_id=(f, below), device_id_type=MESH,
    )
    up = pltpu.make_async_remote_copy(
        src_ref=held.at[1:3, 48:96], dst_ref=held.at[1:3, 144:192], send_sem=halo_send.at[1],
        recv_sem=halo_recv.at[1], device_id=(f, above), device_id_type=MESH,
    )

    @pl.when(jnp.logical_not(below_later))
    def _():
        down.start()

    @pl.when(jnp.logical_not(above_later))
    def _():
        up.start()

    fetch.wait()
    gains.wait()

    def fold(step, carry):
        at = pl.multiple_of(step * 16, 16)
        for half in range(2):
            lanes = slice(128 * half, 128 * half + 128)
            for kind in range(3):
                def tap(h, w):
                    if kind == 0:
                        return raw[h * 3 + w, pl.ds(at, 16), lanes].astype(F32) + raw[
                            9 + h * 3 + w, pl.ds(at, 16), lanes].astype(F32)
                    return raw[(18 if kind == 1 else 9) + h * 3 + w, pl.ds(at, 16), lanes].astype(F32)

                t = [[tap(h, w) for w in range(3)] for h in range(3)]
                by_row = [[t[0], [t[1][w] + t[2][w] for w in range(3)]],
                          [[t[0][w] + t[1][w] for w in range(3)], t[2]]]
                for p in range(2):
                    for a in range(2):
                        u = by_row[p][a]
                        by_col = [[u[0], u[1] + u[2]], [u[0] + u[1], u[2]]]
                        for q in range(2):
                            for b in range(2):
                                base = kind * 1024 + (a * 2 + b) * 256
                                folded[p * 2 + q, pl.ds(base + at, 16), lanes] = by_col[q][b].astype(BF16)
        return carry

    lax.fori_loop(0, 16, fold, 0)

    @pl.when(below_later)
    def _():
        up.wait_recv()
        down.start()

    @pl.when(above_later)
    def _():
        down.wait_recv()
        up.start()

    @pl.when(jnp.logical_not(below_later))
    def _():
        up.wait_recv()

    @pl.when(jnp.logical_not(above_later))
    def _():
        down.wait_recv()

    forward = pltpu.make_async_remote_copy(
        src_ref=held.at[2], dst_ref=held.at[0], send_sem=halo_send.at[2], recv_sem=halo_recv.at[2],
        device_id=((f + 1) % frames, r), device_id_type=MESH,
    )

    def pass_on():
        @pl.when(f + 1 < frames)
        def _():
            forward.start()

        @pl.when(f > 0)
        def _():
            forward.wait_recv()

        @pl.when(f == 0)
        def _():
            held[0] = held[1]

        halo_out[...] = held[...]

    others = buf1.at[ROOT, 0:rows - 1]

    @pl.when(is_hub)
    def _():
        is_mean = (lane_index((1, 128)) & 3) < 2
        pivot = jnp.where(is_mean, mine, 0.0)

        def arrived(k):
            @pl.when(k != f)
            def _():
                pltpu.make_async_copy(buf1.at[k], buf1.at[k], recv1.at[k]).wait()

            @pl.when(k == f)
            def _():
                pltpu.make_async_copy(others, others, recv1.at[k]).wait()

            @pl.when(is_root & (k > ROOT + 1))
            def _():
                pl.semaphore_signal(ready, inc=1, device_id=(k - 1, r), device_id_type=MESH)

        def collect(k, carry):
            arrived(k)
            return carry

        lax.fori_loop(0, ROOT + 2, collect, 0)

        @pl.when(is_root)
        def _():
            pass_on()

        lax.fori_loop(ROOT + 2, frames - LATE, collect, 0)

        @pl.when(is_aide)
        def _():
            pl.semaphore_wait(ready, 1)
            pass_on()

        for k in range(frames - LATE, frames):
            pltpu.make_async_copy(buf1.at[k], buf1.at[k], recv1.at[k]).wait()

            @pl.when(is_root)
            def _():
                pl.semaphore_signal(ready, inc=1, device_id=(k - 1, r), device_id_type=MESH)

        shares = (buf1[...] - pivot).reshape(frames * rows // 8, 8, 128)
        sums = jnp.sum(shares, axis=0), jnp.sum(jnp.square(shares), axis=0)
        offset = jnp.sum(sums[0], axis=0, keepdims=True)
        share = offset * (1.0 / (frames * rows))
        final[0, 0:1] = jnp.where(is_mean, pivot + share, offset)
        final[0, 1:2] = jnp.sum(sums[1], axis=0, keepdims=True) - offset * share

    @pl.when(passes_on)
    def _():
        def send_third(k, carry):
            @pl.when((k != ROOT) & (k != f))
            def _():
                pltpu.make_async_remote_copy(
                    src_ref=final.at[0], dst_ref=final.at[0], send_sem=send3, recv_sem=recv3,
                    device_id=(k, r), device_id_type=MESH,
                ).start()

            return carry

        lax.fori_loop(0, frames, send_third, 0)

    @pl.when(jnp.logical_not(is_hub))
    def _():
        @pl.when((f > ROOT) & (f + 1 < frames))
        def _():
            pl.semaphore_wait(ready, 1)

        pass_on()
        pltpu.make_async_copy(final.at[0], final.at[0], recv3).wait()

    kind = lane_index((8, 128)) & 3
    line, apart = (quad(jnp.broadcast_to(final[0, i:i + 1], (8, 128))) for i in range(2))

    def everywhere(near, k):
        v = near[0]
        for distance in range(1, 4):
            v = jnp.where((kind ^ k) == distance, near[distance], v)
        return v[0:1]

    spread = [everywhere(line, 0), everywhere(line, 1)]
    spread += [everywhere(line, 2 + h) + 192.0 * GROUP * everywhere(apart, h) for h in range(2)]
    var = jnp.concatenate(spread[2:], axis=1) * (1.0 / total)
    stat_out[0:1] = jnp.concatenate(spread[:2], axis=1)
    stat_out[1:2] = lax.rsqrt(var + 1e-06) * scale[...]

    @pl.when(jnp.logical_not(is_hub))
    def _():
        everyone = buf1.at[0, 0:1]
        pltpu.make_async_copy(everyone, everyone, send1).wait()

    every_root = buf1.at[0]
    pltpu.make_async_copy(every_root, every_root, send1).wait()

    @pl.when(passes_on)
    def _():
        heard = final.at[0:frames - 2]
        pltpu.make_async_copy(heard, heard, send3).wait()

    @pl.when(passes_on & is_root)
    def _():
        pltpu.make_async_copy(final.at[0], final.at[0], send3).wait()

    down.wait_send()
    up.wait_send()

    @pl.when(f + 1 < frames)
    def _():
        forward.wait_send()


def conv_kernel(shape, halo, stat, folded, out, act, even_rows, odd_rows, wide, staged, out_sem):
    rows = shape
    r = lax.axis_index("row")

    mean, scale = stat[0:1], stat[1:2]
    for t in range(3):
        v = (halo[t, :, :].astype(F32)[24:168] - mean) * scale
        v = (v / (1.0 + jnp.exp(-v))).astype(BF16).astype(F32).reshape(6, 24, 256)
        top = jnp.where(r == 0, v[1:2], v[0:1])
        bottom = jnp.where(r == rows - 1, v[4:5], v[5:6])
        v = jnp.concatenate([top, v[1:5], bottom], axis=0)
        act[t, :, 8:32, :] = v
        act[t, :, 7:8, :] = v[:, 0:1]
        act[t, :, 32:33, :] = v[:, 23:24]
    for s in range(3):
        v = [act[t, :, 7 + s:31 + s, :] for t in range(3)]
        v = v + [v[1] - v[0], v[2] - v[1]]
        for t in range(5):
            even_rows[s, t] = v[t].reshape(144, 256).astype(BF16)
            odd_rows[s, t] = v[t][1:5].reshape(96, 256).astype(BF16)

    def piece(kind, sr, sc):
        first = (0, 1, 3)[kind]
        if sr == 1:
            return odd_rows[sc, first:first + 2].reshape(192, 256)
        return even_rows[sc, first:first + 2, 24 * sr:24 * sr + 96].reshape(192, 256)

    copies = []
    for p in range(2):
        for q in range(2):
            def product(kinds):
                total = None
                for kind in kinds:
                    for a in range(2):
                        for b in range(2):
                            at = kind * 1024 + (a * 2 + b) * 256
                            term = jnp.dot(piece(kind, p + a, q + b), folded[p * 2 + q, at:at + 256],
                                           preferred_element_type=F32)
                            total = term if total is None else total + term
                return total

            first, step = product((0, 1)), product((2,))
            second = first + step
            for i in range(2):
                for alpha, v in enumerate((first, second)):
                    t = 2 * i + alpha
                    for half in range(2):
                        lanes = slice(128 * half, 128 * half + 128)
                        wide[half, t, :, pl.ds(q, 24, 2), :] = v[96 * i:96 * i + 96, lanes].reshape(4, 24, 128)
                        if q == 1:
                            staged[p, t, :, :, lanes] = wide[half, t, :, 0:48].astype(BF16)
                    if q == 1 and (p == 1 or t == 3):
                        part = slice(t, t + 1) if p == 1 else slice(0, 4)
                        copy = pltpu.make_async_copy(staged.at[p, part], out.at[part, :, p], out_sem.at[p, t])
                        copy.start()
                        copies.append(copy)
    for copy in copies:
        copy.wait()


def solution(mesh):
    frames, rows = mesh.shape["frame"], mesh.shape["row"]
    xdim = 4 if rows % 4 == 0 else 1
    any_, vmem = pl.BlockSpec(memory_space=pltpu.HBM), pl.BlockSpec(memory_space=pltpu.VMEM)

    def shards(features, norm_gain, conv_up):
        voxels = float(192 * GROUP * frames * rows)
        halo, stat, folded = pl.pallas_call(
            functools.partial(comm_kernel, (frames, rows // xdim, xdim, voxels)),
            out_shape=(pltpu.VMEM((3, 192, 256), BF16), pltpu.VMEM((2, 256), F32), pltpu.VMEM((4, 3072, 256), BF16)),
            in_specs=[any_, any_, any_],
            out_specs=(vmem, vmem, vmem),
            scratch_shapes=[
                pltpu.VMEM((27, 256, 256), BF16),
                pltpu.VMEM((3, 192, 256), BF16),
                pltpu.VMEM((1, 256), F32),
                pltpu.VMEM((1, 128), F32),
                pltpu.VMEM((frames, rows, 128), F32),
                pltpu.VMEM((frames - 1, 2, 128), F32),
                pltpu.SemaphoreType.DMA((6,)),
                pltpu.SemaphoreType.DMA,
                pltpu.SemaphoreType.DMA((frames,)),
                pltpu.SemaphoreType.DMA,
                pltpu.SemaphoreType.DMA,
                pltpu.SemaphoreType.DMA((3,)),
                pltpu.SemaphoreType.DMA((3,)),
                pltpu.SemaphoreType.REGULAR,
            ],
            compiler_params=pltpu.CompilerParams(
                collective_id=0, has_side_effects=True, vmem_limit_bytes=54 * 2**20),
            name="statistics",
        )(features.reshape(2, 96, 256), conv_up.reshape(27, 256, 256), norm_gain.reshape(1, 256))
        out = pl.pallas_call(
            functools.partial(conv_kernel, rows),
            out_shape=jax.ShapeDtypeStruct((4, 4, 2, 48, 256), BF16),
            in_specs=[vmem, vmem, vmem],
            out_specs=any_,
            scratch_shapes=[
                pltpu.VMEM((3, 6, 40, 256), F32),
                pltpu.VMEM((3, 5, 144, 256), BF16),
                pltpu.VMEM((3, 5, 96, 256), BF16),
                pltpu.VMEM((2, 4, 4, 56, 128), F32),
                pltpu.VMEM((2, 4, 4, 48, 256), BF16),
                pltpu.SemaphoreType.DMA((2, 4)),
            ],
            compiler_params=pltpu.CompilerParams(vmem_limit_bytes=24 * 2**20),
            name="conv",
        )(halo, stat, folded)
        return out.reshape(4, 8, 48, 256)

    spec = P("frame", "row", None, None)
    return jax.shard_map(shards, mesh=mesh, in_specs=(spec, P(), P()), out_specs=spec, check_vma=False)
```

```python
import functools

import jax
import jax.numpy as jnp
from jax import lax
from jax.experimental import pallas as pl
from jax.experimental.pallas import tpu as pltpu
from jax.sharding import PartitionSpec as P

MESH = pl.DeviceIdType.MESH
GROUP = 8
F32, BF16 = jnp.float32, jnp.bfloat16
ROOT, AIDE = 1, 3
LATE = 8


def lane_index(shape):
    return lax.broadcasted_iota(jnp.int32, shape, len(shape) - 1)


def swapped(value, distance):
    upper = (lane_index(value.shape) & distance) == 0
    return jnp.where(upper, pltpu.roll(value, 128 - distance, 1), pltpu.roll(value, distance, 1))


def quad(value):
    lane = lane_index(value.shape) & 3
    after = [pltpu.roll(value, 128 - d, 1) for d in (1, 2, 3)]
    before = [pltpu.roll(value, d, 1) for d in (1, 2, 3)]
    one = jnp.where((lane & 1) == 0, after[0], before[0])
    two = jnp.where(lane < 2, after[1], before[1])
    three = jnp.where(lane == 0, after[2], jnp.where(lane == 3, before[2], jnp.where(lane == 1, after[0], before[0])))
    return value, one, two, three


def local_statistics(own, rows):
    count = float(rows)
    pivot = own[0:1]
    apart = own - pivot
    offset = jnp.sum(apart, axis=0, keepdims=True)
    spread = jnp.sum(jnp.square(apart), axis=0, keepdims=True) - offset * offset * (1.0 / count)
    mean = pivot + offset * (1.0 / count)
    low = lax.broadcasted_iota(jnp.int32, (8, 128), 0) == 0

    def halves(v):
        return jnp.where(low, jnp.broadcast_to(v[:, 0:128], (8, 128)), jnp.broadcast_to(v[:, 128:256], (8, 128)))

    m, s = halves(mean), halves(spread)
    lane = lane_index((8, 128)) & (GROUP - 1)
    shifts = [(d, lane >= d) for d in range(1, GROUP)] + [(128 - d, lane + d < GROUP) for d in range(1, GROUP)]
    rolled = [pltpu.roll(m, d, 1) for d, _ in shifts]
    s = s + sum(jnp.where(inside, pltpu.roll(s, d, 1), 0.0) for d, inside in shifts)
    center = (m + sum(jnp.where(inside, v, 0.0) for (_, inside), v in zip(shifts, rolled))) * (1.0 / GROUP)
    apart = sum(jnp.where(inside, jnp.square(v - center), 0.0) for (_, inside), v in zip(shifts, rolled))
    s = s + count * (jnp.square(m - center) + apart)
    m = center
    kind = lane_index((1, 128)) & 3
    return jnp.where(kind == 0, m[0:1], jnp.where(kind == 1, m[1:2], jnp.where(kind == 2, s[0:1], s[1:2])))


def comm_kernel(
    shape, feat, weight, gain, halo_out, stat_out, folded,
    raw, held, scale, msg1, buf1, final,
    in_sem, send1, recv1, send3, recv3, halo_send, halo_recv, ready,
):
    frames, ydim, xdim, total = shape
    rows = ydim * xdim
    f, r = lax.axis_index("frame"), lax.axis_index("row")
    y, x = r // xdim, r % xdim
    is_root = f == ROOT
    is_aide = (f == AIDE) & (r == 0)
    is_hub = is_root | is_aide
    passes_on = (is_root & (r > 0)) | is_aide

    loads = [
        pltpu.make_async_copy(feat.at[t, part], held.at[1 + t, pl.ds(48 + part.start, 48)], in_sem.at[2 + 2 * t + i])
        for t in range(2) for i, part in enumerate((slice(0, 48), slice(48, 96)))
    ]
    for load in loads:
        load.start()

    def order(row):
        return row % xdim * rows + row

    below, above = (r + 1) % rows, (r + rows - 1) % rows
    below_later, above_later = order(below) > order(r), order(above) > order(r)

    def plane(i):
        return ((y + i // xdim) % ydim) * xdim + (x + i) % xdim

    def share_to(frame, row):
        return pltpu.make_async_remote_copy(
            src_ref=msg1, dst_ref=buf1.at[f, pl.ds(r, 1)], send_sem=send1, recv_sem=recv1.at[f],
            device_id=(frame, row), device_id_type=MESH,
        )

    barrier = pltpu.get_barrier_semaphore()

    def greet(frame, row):
        pl.semaphore_signal(barrier, inc=1, device_id=(frame, row), device_id_type=MESH)

    def greet_plane(i, carry):
        greet(f, plane(i))
        return carry

    def greet_line(k, carry):
        greet(k, r)
        return carry

    @pl.when(is_root)
    def _():
        lax.fori_loop(1, rows, greet_plane, 0)

    @pl.when(jnp.logical_not(is_root))
    def _():
        @pl.when(below_later)
        def _():
            greet(f, below)

        @pl.when(above_later)
        def _():
            greet(f, above)

    @pl.when(is_aide)
    def _():
        def greet_root(k, carry):
            greet(ROOT, k)
            return carry

        lax.fori_loop(0, rows, greet_root, 0)

    for load in loads:
        load.wait()
    values = held[1:3, 48:144].astype(F32).reshape(192, 256)
    mine = local_statistics(values, 192)
    msg1[...] = mine
    pl.semaphore_wait(barrier, jnp.where(
        is_root, rows, 3 - below_later.astype(jnp.int32) - above_later.astype(jnp.int32)))

    @pl.when(is_root)
    def _():
        greet(0, r)
        lax.fori_loop(ROOT + 1, frames, greet_line, 0)

    @pl.when(is_hub)
    def _():
        buf1[f, pl.ds(r, 1)] = mine

    @pl.when(jnp.logical_not(is_root))
    def _():
        share_to(ROOT, r).start()

    def to_roots(i, carry):
        share_to(ROOT, plane(i)).start()
        return carry

    lax.fori_loop(rows // 2, rows, to_roots, 0)

    @pl.when(jnp.logical_not(is_aide))
    def _():
        share_to(AIDE, 0).start()

    lax.fori_loop(1, rows // 2, to_roots, 0)

    fetch = pltpu.make_async_copy(weight, raw, in_sem.at[0])
    fetch.start()
    gains = pltpu.make_async_copy(gain, scale, in_sem.at[1])
    gains.start()

    down = pltpu.make_async_remote_copy(
        src_ref=held.at[1:3, 96:144], dst_ref=held.at[1:3, 0:48], send_sem=halo_send.at[0],
        recv_sem=halo_recv.at[0], device_id=(f, below), device_id_type=MESH,
    )
    up = pltpu.make_async_remote_copy(
        src_ref=held.at[1:3, 48:96], dst_ref=held.at[1:3, 144:192], send_sem=halo_send.at[1],
        recv_sem=halo_recv.at[1], device_id=(f, above), device_id_type=MESH,
    )

    @pl.when(jnp.logical_not(below_later))
    def _():
        down.start()

    @pl.when(jnp.logical_not(above_later))
    def _():
        up.start()

    fetch.wait()
    gains.wait()

    def fold(step, carry):
        at = pl.multiple_of(step * 16, 16)
        for half in range(2):
            lanes = slice(128 * half, 128 * half + 128)
            for kind in range(3):
                def tap(h, w):
                    if kind == 0:
                        return raw[h * 3 + w, pl.ds(at, 16), lanes].astype(F32) + raw[
                            9 + h * 3 + w, pl.ds(at, 16), lanes].astype(F32)
                    return raw[(18 if kind == 1 else 9) + h * 3 + w, pl.ds(at, 16), lanes].astype(F32)

                t = [[tap(h, w) for w in range(3)] for h in range(3)]
                by_row = [[t[0], [t[1][w] + t[2][w] for w in range(3)]],
                          [[t[0][w] + t[1][w] for w in range(3)], t[2]]]
                for p in range(2):
                    for a in range(2):
                        u = by_row[p][a]
                        by_col = [[u[0], u[1] + u[2]], [u[0] + u[1], u[2]]]
                        for q in range(2):
                            for b in range(2):
                                base = kind * 1024 + (a * 2 + b) * 256
                                folded[p * 2 + q, pl.ds(base + at, 16), lanes] = by_col[q][b].astype(BF16)
        return carry

    lax.fori_loop(0, 16, fold, 0)

    @pl.when(below_later)
    def _():
        up.wait_recv()
        down.start()

    @pl.when(above_later)
    def _():
        down.wait_recv()
        up.start()

    @pl.when(jnp.logical_not(below_later))
    def _():
        up.wait_recv()

    @pl.when(jnp.logical_not(above_later))
    def _():
        down.wait_recv()

    forward = pltpu.make_async_remote_copy(
        src_ref=held.at[2], dst_ref=held.at[0], send_sem=halo_send.at[2], recv_sem=halo_recv.at[2],
        device_id=((f + 1) % frames, r), device_id_type=MESH,
    )

    def pass_on():
        @pl.when(f + 1 < frames)
        def _():
            forward.start()

        @pl.when(f > 0)
        def _():
            forward.wait_recv()

        @pl.when(f == 0)
        def _():
            held[0] = held[1]

        halo_out[...] = held[...]

    others = buf1.at[ROOT, 0:rows - 1]

    @pl.when(is_hub)
    def _():
        is_mean = (lane_index((1, 128)) & 3) < 2
        pivot = jnp.where(is_mean, mine, 0.0)

        def arrived(k):
            @pl.when(k != f)
            def _():
                pltpu.make_async_copy(buf1.at[k], buf1.at[k], recv1.at[k]).wait()

            @pl.when(k == f)
            def _():
                pltpu.make_async_copy(others, others, recv1.at[k]).wait()

            @pl.when(is_root & (k > ROOT + 1))
            def _():
                pl.semaphore_signal(ready, inc=1, device_id=(k - 1, r), device_id_type=MESH)

        def collect(k, carry):
            arrived(k)
            return carry

        lax.fori_loop(0, ROOT + 2, collect, 0)

        @pl.when(is_root)
        def _():
            pass_on()

        lax.fori_loop(ROOT + 2, frames - LATE, collect, 0)

        @pl.when(is_aide)
        def _():
            pl.semaphore_wait(ready, 1)
            pass_on()

        for k in range(frames - LATE, frames):
            pltpu.make_async_copy(buf1.at[k], buf1.at[k], recv1.at[k]).wait()

            @pl.when(is_root)
            def _():
                pl.semaphore_signal(ready, inc=1, device_id=(k - 1, r), device_id_type=MESH)

        shares = (buf1[...] - pivot).reshape(frames * rows // 8, 8, 128)
        sums = jnp.sum(shares, axis=0), jnp.sum(jnp.square(shares), axis=0)
        offset = jnp.sum(sums[0], axis=0, keepdims=True)
        share = offset * (1.0 / (frames * rows))
        final[0, 0:1] = jnp.where(is_mean, pivot + share, offset)
        final[0, 1:2] = jnp.sum(sums[1], axis=0, keepdims=True) - offset * share

    @pl.when(passes_on)
    def _():
        def send_third(k, carry):
            @pl.when((k != ROOT) & (k != f))
            def _():
                pltpu.make_async_remote_copy(
                    src_ref=final.at[0], dst_ref=final.at[0], send_sem=send3, recv_sem=recv3,
                    device_id=(k, r), device_id_type=MESH,
                ).start()

            return carry

        lax.fori_loop(0, frames, send_third, 0)

    @pl.when(jnp.logical_not(is_hub))
    def _():
        @pl.when((f > ROOT) & (f + 1 < frames))
        def _():
            pl.semaphore_wait(ready, 1)

        pass_on()
        pltpu.make_async_copy(final.at[0], final.at[0], recv3).wait()

    kind = lane_index((8, 128)) & 3
    line, apart = (quad(jnp.broadcast_to(final[0, i:i + 1], (8, 128))) for i in range(2))

    def everywhere(near, k):
        v = near[0]
        for distance in range(1, 4):
            v = jnp.where((kind ^ k) == distance, near[distance], v)
        return v[0:1]

    spread = [everywhere(line, 0), everywhere(line, 1)]
    spread += [everywhere(line, 2 + h) + 192.0 * GROUP * everywhere(apart, h) for h in range(2)]
    var = jnp.concatenate(spread[2:], axis=1) * (1.0 / total)
    stat_out[0:1] = jnp.concatenate(spread[:2], axis=1)
    stat_out[1:2] = lax.rsqrt(var + 1e-06) * scale[...]

    @pl.when(jnp.logical_not(is_hub))
    def _():
        everyone = buf1.at[0, 0:1]
        pltpu.make_async_copy(everyone, everyone, send1).wait()

    every_root = buf1.at[0]
    pltpu.make_async_copy(every_root, every_root, send1).wait()

    @pl.when(passes_on)
    def _():
        heard = final.at[0:frames - 2]
        pltpu.make_async_copy(heard, heard, send3).wait()

    @pl.when(passes_on & is_root)
    def _():
        pltpu.make_async_copy(final.at[0], final.at[0], send3).wait()

    down.wait_send()
    up.wait_send()

    @pl.when(f + 1 < frames)
    def _():
        forward.wait_send()


def conv_kernel(shape, halo, stat, folded, out, act, even_rows, odd_rows, wide, staged, out_sem):
    rows = shape
    r = lax.axis_index("row")

    mean, scale = stat[0:1], stat[1:2]
    for t in range(3):
        v = (halo[t, :, :].astype(F32)[24:168] - mean) * scale
        v = (v / (1.0 + jnp.exp(-v))).astype(BF16).astype(F32).reshape(6, 24, 256)
        top = jnp.where(r == 0, v[1:2], v[0:1])
        bottom = jnp.where(r == rows - 1, v[4:5], v[5:6])
        v = jnp.concatenate([top, v[1:5], bottom], axis=0)
        act[t, :, 8:32, :] = v
        act[t, :, 7:8, :] = v[:, 0:1]
        act[t, :, 32:33, :] = v[:, 23:24]
    for s in range(3):
        v = [act[t, :, 7 + s:31 + s, :] for t in range(3)]
        v = v + [v[1] - v[0], v[2] - v[1]]
        for t in range(5):
            even_rows[s, t] = v[t].reshape(144, 256).astype(BF16)
            odd_rows[s, t] = v[t][1:5].reshape(96, 256).astype(BF16)

    def piece(kind, sr, sc):
        first = (0, 1, 3)[kind]
        if sr == 1:
            return odd_rows[sc, first:first + 2].reshape(192, 256)
        return even_rows[sc, first:first + 2, 24 * sr:24 * sr + 96].reshape(192, 256)

    copies = []
    for p in range(2):
        for q in range(2):
            def product(kinds):
                total = None
                for kind in kinds:
                    for a in range(2):
                        for b in range(2):
                            at = kind * 1024 + (a * 2 + b) * 256
                            term = jnp.dot(piece(kind, p + a, q + b), folded[p * 2 + q, at:at + 256],
                                           preferred_element_type=F32)
                            total = term if total is None else total + term
                return total

            first, step = product((0, 1)), product((2,))
            second = first + step
            for i in range(2):
                for alpha, v in enumerate((first, second)):
                    t = 2 * i + alpha
                    for half in range(2):
                        lanes = slice(128 * half, 128 * half + 128)
                        wide[half, t, :, pl.ds(q, 24, 2), :] = v[96 * i:96 * i + 96, lanes].reshape(4, 24, 128)
                        if q == 1:
                            staged[p, t, :, :, lanes] = wide[half, t, :, 0:48].astype(BF16)
                    if q == 1 and (p == 1 or t == 3):
                        part = slice(t, t + 1) if p == 1 else slice(0, 4)
                        copy = pltpu.make_async_copy(staged.at[p, part], out.at[part, :, p], out_sem.at[p, t])
                        copy.start()
                        copies.append(copy)
    for copy in copies:
        copy.wait()


def solution(mesh):
    frames, rows = mesh.shape["frame"], mesh.shape["row"]
    xdim = 4 if rows % 4 == 0 else 1
    any_, vmem = pl.BlockSpec(memory_space=pltpu.HBM), pl.BlockSpec(memory_space=pltpu.VMEM)

    def shards(features, norm_gain, conv_up):
        voxels = float(192 * GROUP * frames * rows)
        halo, stat, folded = pl.pallas_call(
            functools.partial(comm_kernel, (frames, rows // xdim, xdim, voxels)),
            out_shape=(pltpu.VMEM((3, 192, 256), BF16), pltpu.VMEM((2, 256), F32), pltpu.VMEM((4, 3072, 256), BF16)),
            in_specs=[any_, any_, any_],
            out_specs=(vmem, vmem, vmem),
            scratch_shapes=[
                pltpu.VMEM((27, 256, 256), BF16),
                pltpu.VMEM((3, 192, 256), BF16),
                pltpu.VMEM((1, 256), F32),
                pltpu.VMEM((1, 128), F32),
                pltpu.VMEM((frames, rows, 128), F32),
                pltpu.VMEM((frames - 1, 2, 128), F32),
                pltpu.SemaphoreType.DMA((6,)),
                pltpu.SemaphoreType.DMA,
                pltpu.SemaphoreType.DMA((frames,)),
                pltpu.SemaphoreType.DMA,
                pltpu.SemaphoreType.DMA,
                pltpu.SemaphoreType.DMA((3,)),
                pltpu.SemaphoreType.DMA((3,)),
                pltpu.SemaphoreType.REGULAR,
            ],
            compiler_params=pltpu.CompilerParams(
                collective_id=0, has_side_effects=True, vmem_limit_bytes=54 * 2**20),
            name="statistics",
        )(features.reshape(2, 96, 256), conv_up.reshape(27, 256, 256), norm_gain.reshape(1, 256))
        out = pl.pallas_call(
            functools.partial(conv_kernel, rows),
            out_shape=jax.ShapeDtypeStruct((4, 4, 2, 48, 256), BF16),
            in_specs=[vmem, vmem, vmem],
            out_specs=any_,
            scratch_shapes=[
                pltpu.VMEM((3, 6, 40, 256), F32),
                pltpu.VMEM((3, 5, 144, 256), BF16),
                pltpu.VMEM((3, 5, 96, 256), BF16),
                pltpu.VMEM((2, 4, 4, 56, 128), F32),
                pltpu.VMEM((2, 4, 4, 48, 256), BF16),
                pltpu.SemaphoreType.DMA((2, 4)),
            ],
            compiler_params=pltpu.CompilerParams(vmem_limit_bytes=24 * 2**20),
            name="conv",
        )(halo, stat, folded)
        return out.reshape(4, 8, 48, 256)

    spec = P("frame", "row", None, None)
    return jax.shard_map(shards, mesh=mesh, in_specs=(spec, P(), P()), out_specs=spec, check_vma=False)
```
